256 devices in a mesh: space: 16 (over x_hi, y, core), band: 16 (over x_lo, z).
Axes of the slice: x: 4 (x_hi: 2, x_lo: 2; x = x_hi * 2 + x_lo), y: 4, z: 8, core: 2. Of those that a mesh axis runs over, the one named last changes fastest.
Arguments:
- orbitals: float32 [384, 64, 4608], P('band', 'space'), may hold values from -6 to 6
- potential: float32 [64, 4608], P('space'), may hold values from -2 to 0
- rotation: bfloat16 [384, 384], replicated, may hold values from -0.3125 to 0.3125
Outputs:
- rotated: float32 [384, 64, 4608], P('band', 'space')
The draws below stay inside these ranges and needn't reach their ends.
All inputs are finite; a program needn't handle non-finite values.
Results may differ from the reference program's by a relative error of at most 0.0029.
Values may be sent and summed in bfloat16 or wider, within the bound.
No kernel may reach another device: no remote copies, remote signals or barrier semaphores. Data moves between devices by JAX's collectives and lax.ppermute only.
A program may use at most 128 MiB of HBM per device.

```python
import jax
import jax.numpy as jnp
from jax import lax

NB = 384
NY = 48
NZ = 96
DEGREE = 4
NX = 64


def shard_levels(stream_key, extent, cuts, smallest, top_value):
    def one(axis_at, parts):
        heights = jax.random.uniform(jax.random.fold_in(jax.random.fold_in(stream_key, 6), axis_at), (parts,), jnp.float32, smallest / len(cuts), top_value / len(cuts))
        return jnp.repeat(jnp.exp(heights), extent[axis_at] // parts).reshape((-1,) + (1,) * (len(extent) - axis_at - 1))

    factor_of = one(*cuts[0])
    for cut in cuts[1:]:
        factor_of = factor_of * one(*cut)
    return factor_of


def scatter_about(stream_key, dims, spread, bound, shards=(), dtype=jnp.bfloat16):
    array = jax.random.normal(stream_key, dims, jnp.float32) * spread
    if len(shards) > 0:
        array = shard_levels(stream_key, dims, shards, -0.22, 0.18) * array
    return jnp.clip(array, min=-bound, max=bound).astype(dtype)


def setup_inputs(seed: int = 0) -> dict:
    splits = jax.random.split(jax.random.key(seed), 4)
    return {
        "orbitals": scatter_about(splits[0], (NB, NX, NY * NZ), 1.0, 6.0, ((0, 16), (1, 16)), jnp.float32),
        "potential": jnp.clip(-2.0 + 2.0 * jax.random.uniform(splits[1], (NX, NY * NZ), jnp.float32) ** shard_levels(splits[1], (NX, NY * NZ), ((0, 16),), -0.2, 0.2), -2.0, 0.0),
        "rotation": scatter_about(splits[2], (NB, NB), NB ** -0.5, 0.3125),
    }


center_value = 4.75
half_width = 3.75


def apply_hamiltonian(padded, potential):
    center = padded[:, 2:-2]
    planes = center.shape[1]
    columns = center.shape[2]
    laplace = -7.5 * center
    laplace = laplace + (4.0 / 3.0) * (padded[:, 1:planes + 1] + padded[:, 3:planes + 3])
    laplace = laplace - (1.0 / 12.0) * (padded[:, 0:planes] + padded[:, 4:planes + 4])
    shifted_y = jnp.pad(center, ((0, 0), (0, 0), (2 * NZ, 2 * NZ)))
    laplace = laplace + (4.0 / 3.0) * (shifted_y[:, :, NZ:NZ + columns] + shifted_y[:, :, 3 * NZ:3 * NZ + columns])
    laplace = laplace - (1.0 / 12.0) * (shifted_y[:, :, 0:columns] + shifted_y[:, :, 4 * NZ:4 * NZ + columns])
    z_index = jnp.arange(columns) % NZ
    shifted_z = jnp.pad(center, ((0, 0), (0, 0), (2, 2)))
    minus_one = shifted_z[:, :, 1:columns + 1] * jnp.where(z_index >= 1, 1.0, 0.0)
    plus_one = shifted_z[:, :, 3:columns + 3] * jnp.where(z_index <= NZ - 2, 1.0, 0.0)
    minus_two = shifted_z[:, :, 0:columns] * jnp.where(z_index >= 2, 1.0, 0.0)
    plus_two = shifted_z[:, :, 4:columns + 4] * jnp.where(z_index <= NZ - 3, 1.0, 0.0)
    laplace = laplace + (4.0 / 3.0) * (minus_one + plus_one) - (1.0 / 12.0) * (minus_two + plus_two)
    return -0.5 * laplace + potential * center


def filter_block(block, potential):
    def step_once(current):
        padded = jnp.pad(current, ((0, 0), (2, 2), (0, 0)))
        return apply_hamiltonian(padded, potential) - center_value * current

    previous = block
    current = step_once(block) / half_width
    for degree in range(DEGREE - 1):
        following = (2.0 / half_width) * step_once(current) - previous
        previous = current
        current = following
    return current


def reference(orbitals, potential, rotation):
    blocks = orbitals.reshape(8, NB // 8, NX, NY * NZ)
    result = lax.map(lambda block: filter_block(block, potential), blocks)
    filtered = result.reshape(NB, NX * NY * NZ).astype(jnp.bfloat16)
    rotated = jnp.dot(rotation.T, filtered, preferred_element_type=jnp.float32)
    return rotated.reshape(NB, NX, NY * NZ)
```

```python
import jax
import jax.numpy as jnp
from jax import lax
from jax.sharding import PartitionSpec as P

NZ = 96
DEGREE = 4


center_value = 4.75
half_width = 3.75


def with_halo(cells, sides, width):
    for axis, dim in sides:
        count = lax.axis_size(axis)
        ends = count - 1
        head = lax.slice_in_dim(cells, 0, width, axis=dim)
        tail = lax.slice_in_dim(cells, cells.shape[dim] - width, cells.shape[dim], axis=dim)
        cells = jnp.concatenate(
            [
                lax.ppermute(tail, axis, [(i, (i + 1) % count) for i in range(ends)]),
                cells,
                lax.ppermute(head, axis, [((i + 1) % count, i) for i in range(ends)]),
            ],
            axis=dim,
        )
    return cells


def apply_hamiltonian(padded, potential):
    center = padded[:, 2:-2]
    planes = center.shape[1]
    columns = center.shape[2]
    laplace = -7.5 * center
    laplace = laplace + 4.0 / 3.0 * (padded[:, 1 : planes + 1] + padded[:, 3 : planes + 3])
    laplace = laplace - 1.0 / 12.0 * (padded[:, 0:planes] + padded[:, 4 : planes + 4])
    shifted_y = jnp.pad(center, ((0, 0), (0, 0), (2 * NZ, 2 * NZ)))
    laplace = laplace + 4.0 / 3.0 * (
        shifted_y[:, :, NZ : NZ + columns] + shifted_y[:, :, 3 * NZ : 3 * NZ + columns]
    )
    laplace = laplace - 1.0 / 12.0 * (
        shifted_y[:, :, 0:columns] + shifted_y[:, :, 4 * NZ : 4 * NZ + columns]
    )
    z_index = jnp.arange(columns) % NZ
    shifted_z = jnp.pad(center, ((0, 0), (0, 0), (2, 2)))
    minus_one = shifted_z[:, :, 1 : columns + 1] * jnp.where(z_index >= 1, 1.0, 0.0)
    plus_one = shifted_z[:, :, 3 : columns + 3] * jnp.where(z_index <= NZ - 2, 1.0, 0.0)
    minus_two = shifted_z[:, :, 0:columns] * jnp.where(z_index >= 2, 1.0, 0.0)
    plus_two = shifted_z[:, :, 4 : columns + 4] * jnp.where(z_index <= NZ - 3, 1.0, 0.0)
    laplace = laplace + 4.0 / 3.0 * (minus_one + plus_one) - 1.0 / 12.0 * (minus_two + plus_two)
    return -0.5 * laplace + potential * center


def step_once(current, potential):
    padded = with_halo(current, (("space", 1),), 2)
    return apply_hamiltonian(padded, potential) - center_value * current


def body(orbitals, potential, rotation):
    previous = orbitals
    current = step_once(orbitals, potential) / half_width
    for degree in range(DEGREE - 1):
        following = 2.0 / half_width * step_once(current, potential) - previous
        previous = current
        current = following
    filtered = current.astype(jnp.bfloat16)
    own, planes, columns = filtered.shape
    members = lax.axis_size("band")
    parts = members // planes
    width = columns // parts
    by_cells = filtered.reshape(own, planes, parts, width).transpose(1, 2, 0, 3)
    by_cells = by_cells.reshape(members, own, width)
    every = lax.all_to_all(by_cells, "band", 0, 0)
    every = every.reshape(members * own, width)
    summed = jnp.dot(rotation.T, every, preferred_element_type=jnp.float32)
    summed = summed.astype(jnp.bfloat16).reshape(members, own, width)
    back = lax.all_to_all(summed, "band", 0, 0)
    back = back.reshape(planes, parts, own, width).transpose(2, 0, 1, 3)
    return back.reshape(own, planes, columns).astype(jnp.float32)


def solution(mesh):
    return jax.shard_map(
        body,
        mesh=mesh,
        in_specs=(P("band", "space", None), P("space", None), P()),
        out_specs=P("band", "space", None),
        check_vma=False,
    )
```

```python
import functools

import jax
import jax.numpy as jnp
import numpy as np
from jax import lax
from jax.experimental import pallas as pl
from jax.experimental.pallas import tpu as pltpu
from jax.sharding import PartitionSpec as P

NY = 48
NZ = 96
LANE = 128
ROWS = 8
GROUPS = 4
RUNS = NY // GROUPS
ZI = 3
ZB = NZ // ZI
PIECES = RUNS * ZI

CENTER = 4.75
HALF_WIDTH = 3.75
NEAR = -2.0 / 3.0 / HALF_WIDTH
FAR = 1.0 / 24.0 / HALF_WIDTH

CHUNKS = (24,)


def lanes_of(rows):
    return lax.broadcasted_iota(jnp.int32, (rows, LANE), 1)


def piece(j):
    return pl.ds(j * LANE, LANE)


def pick(values, lanes):
    return jnp.take_along_axis(values, lanes, axis=1)


def to_runs_kernel(cells, out):
    planes, rows, _ = out.shape
    lane = lanes_of(rows)
    group = lane // ZB

    def one_plane(p, _):
        for b in range(RUNS):
            for zi in range(ZI):
                total = None
                for a in range(GROUPS):
                    start = (RUNS * a + b) * NZ
                    j, offset = start // LANE, start % LANE
                    source = lane % ZB * ZI + (offset + zi)
                    part = pick(cells[p, :, piece(j)], source % LANE)
                    if offset + NZ > LANE:
                        part = jnp.where(source < LANE, part, pick(cells[p, :, piece(j + 1)], source % LANE))
                    total = part if total is None else jnp.where(group == a, part, total)
                out[p, :, piece(ZI * b + zi)] = total
        return 0

    lax.fori_loop(0, planes, one_plane, 0)


def to_runs(cells):
    planes, count, columns = cells.shape
    rows = min(count, ROWS)
    spec = pl.BlockSpec((planes, rows, columns), lambda i: (0, i, 0))
    return pl.pallas_call(
        to_runs_kernel,
        grid=(count // rows,),
        in_specs=[spec],
        out_specs=spec,
        out_shape=jax.ShapeDtypeStruct(cells.shape, cells.dtype),
        compiler_params=pltpu.CompilerParams(vmem_limit_bytes=32 * 1024 * 1024),
        cost_estimate=pl.CostEstimate(flops=40000 * count * columns, bytes_accessed=cells.size * 8, transcendentals=0),
    )(cells)


def stencil_row(src, plane, masks, emit):
    a_last, a_first, zb_last, zb_first = masks
    centers, turned = {}, {}

    def center(b, zi):
        if (b, zi) not in centers:
            centers[b, zi] = src[plane + 2, :, piece(ZI * b + zi)]
        return centers[b, zi]

    def turn(b, zi, by, mask):
        if (b, zi, by) not in turned:
            turned[b, zi, by] = jnp.where(mask, 0.0, pltpu.roll(center(b, zi), by, 1))
        return turned[b, zi, by]

    def at_y(b, zi):
        if b < 0:
            return turn(b + RUNS, zi, ZB, a_first)
        if b >= RUNS:
            return turn(b - RUNS, zi, LANE - ZB, a_last)
        return center(b, zi)

    def at_z(b, zi):
        if zi < 0:
            return turn(b, zi + ZI, 1, zb_first)
        if zi >= ZI:
            return turn(b, zi - ZI, LANE - 1, zb_last)
        return center(b, zi)

    def at_x(j, k):
        return src[plane + 2 + k, :, piece(j)]

    for b in range(RUNS):
        for zi in range(ZI):
            j = ZI * b + zi
            near, far = [
                (at_x(j, -k) + at_x(j, k)) + (at_y(b - k, zi) + at_y(b + k, zi)) + (at_z(b, zi - k) + at_z(b, zi + k))
                for k in (1, 2)
            ]
            emit(j, center(b, zi), near, far)


def split_groups(four, odd, upper):
    half = {}
    for i in (0, 2):
        half[i] = jnp.where(odd, pltpu.roll(four[i + 1], ZB, 1), four[i])
        half[i + 1] = jnp.where(odd, four[i + 1], pltpu.roll(four[i], LANE - ZB, 1))
    done = {}
    for i in (0, 1):
        done[i] = jnp.where(upper, pltpu.roll(half[i + 2], 2 * ZB, 1), half[i])
        done[i + 2] = jnp.where(upper, half[i + 2], pltpu.roll(half[i], 2 * ZB, 1))
    return done


def two_steps_kernel(last, inside, lo, own, hi, potential, *rest):
    if last:
        first, out, field, inner, diag = rest
    else:
        out, field, inner, diag = rest
    planes, rows, columns = own.shape

    @pl.when(pl.program_id(0) == 0)
    def _():
        for p in range(planes + 4):
            scaled = (potential[p : p + 1, :] + (HALF_WIDTH - CENTER)) / HALF_WIDTH
            diag[p] = jnp.broadcast_to(scaled, (rows, columns))

    field[0:planes] = lo[...]
    field[planes : 2 * planes] = own[...]
    field[2 * planes : 3 * planes] = hi[...]

    lane = lanes_of(rows)
    masks = (lane >= LANE - ZB, lane < ZB, lane % ZB == ZB - 1, lane % ZB == 0)
    odd = lane // ZB % 2 == 1
    upper = lane >= 2 * ZB

    def first_stage(p, _):
        here = jnp.where(p < 2, inside[0], jnp.where(p >= planes + 2, inside[1], 1.0))
        near_by = here * NEAR
        far_by = here * FAR

        def emit(j, center, near, far):
            inner[p, :, piece(j)] = diag[p, :, piece(j)] * center + near_by * near + far_by * far

        stencil_row(field, p + planes - 4, masks, emit)
        return 0

    lax.fori_loop(0, planes + 4, first_stage, 0)

    def second_stage(p, _):
        held = []

        def emit(j, center, near, far):
            total = diag[p + 2, :, piece(j)] * center + NEAR * near + FAR * far
            total = 2.0 * total - field[p + planes, :, piece(j)]
            if not last:
                out[p, :, piece(j)] = total
                return
            held.append(2.0 * total - first[p, :, piece(j)])
            if len(held) == GROUPS:
                done = split_groups(held, odd, upper)
                for a in range(GROUPS):
                    out[GROUPS * p + a, :, piece(j // GROUPS)] = done[a]
                held.clear()

        stencil_row(inner, p, masks, emit)
        return 0

    lax.fori_loop(0, planes, second_stage, 0)


def two_steps(inside, lo, own, hi, potential, first=None):
    planes, count, columns = own.shape
    last = first is not None
    spec = pl.BlockSpec((planes, ROWS, columns), lambda i: (0, i, 0))
    out_shape, out_spec = (planes, count, columns), spec
    if last:
        width = columns // GROUPS
        out_shape = (planes * GROUPS, count, width)
        out_spec = pl.BlockSpec((planes * GROUPS, ROWS, width), lambda i: (0, i, 0))
    return pl.pallas_call(
        functools.partial(two_steps_kernel, last),
        grid=(count // ROWS,),
        in_specs=[
            pl.BlockSpec(memory_space=pltpu.SMEM),
            spec,
            spec,
            spec,
            pl.BlockSpec(potential.shape, lambda i: (0, 0)),
        ]
        + [spec] * last,
        out_specs=out_spec,
        out_shape=jax.ShapeDtypeStruct(out_shape, jnp.float32),
        scratch_shapes=[
            pltpu.VMEM((planes * 3, ROWS, columns), jnp.float32),
            pltpu.VMEM((planes + 4, ROWS, columns), jnp.float32),
            pltpu.VMEM((planes + 4, ROWS, columns), jnp.float32),
        ],
        compiler_params=pltpu.CompilerParams(vmem_limit_bytes=32 * 1024 * 1024),
        cost_estimate=pl.CostEstimate(flops=80000 * count * columns, bytes_accessed=own.size * 16, transcendentals=0),
    )(inside, lo, own, hi, potential, *([first] if last else []))


def z_order():
    one = np.zeros((NZ, NZ), np.float32)
    for z in range(NZ):
        one[z % ZI * ZB + z // ZI, z] = 1.0
    return jnp.asarray(np.kron(np.eye(GROUPS, dtype=np.float32), one), jnp.bfloat16)


def body(orbitals, potential, rotation):
    count, planes, columns = orbitals.shape
    domains = lax.axis_size("space")
    members = lax.axis_size("band")
    up = [(i, i + 1) for i in range(domains - 1)]
    down = [(i + 1, i) for i in range(domains - 1)]

    def around(cells):
        return lax.ppermute(cells, "space", up), lax.ppermute(cells, "space", down)

    at = lax.axis_index("space")
    inside = jnp.stack([at > 0, at < domains - 1]).astype(jnp.float32)

    starts = [sum(CHUNKS[:i]) for i in range(len(CHUNKS))]
    pieces = [lax.slice_in_dim(orbitals, s, s + n, axis=0) for s, n in zip(starts, CHUNKS)]
    zeroth = [to_runs(x.transpose(1, 0, 2)) for x in pieces]
    zeroth_around = [around(x) for x in zeroth]

    own_potential = to_runs(potential[None])[0]
    potential_below = lax.ppermute(own_potential[planes - 2 :], "space", up)
    potential_above = lax.ppermute(own_potential[:2], "space", down)
    field = jnp.concatenate([potential_below, own_potential, potential_above], axis=0)

    gathered = []
    second = [two_steps(inside, lo, x, hi, field) for x, (lo, hi) in zip(zeroth, zeroth_around)]
    second_around = [around(x) for x in second]
    for x, y, (lo, hi) in zip(zeroth, second, second_around):
        filtered = two_steps(inside, lo, y, hi, field, first=x).astype(jnp.bfloat16)
        gathered.append(lax.all_to_all(filtered, "band", 0, 0))

    by_member = rotation.reshape(members, count, members * count)
    width = columns // GROUPS
    summed = 0.0
    for s, n, part in zip(starts, CHUNKS, gathered):
        weights = by_member[:, s : s + n].reshape(members * n, members * count)
        summed = summed + jnp.dot(weights.T, part.reshape(members * n, width), preferred_element_type=jnp.float32)
    summed = summed.astype(jnp.bfloat16)
    order = z_order()
    summed = jnp.dot(
        summed.reshape(-1, order.shape[0]), order, preferred_element_type=jnp.float32
    ).astype(jnp.bfloat16)
    back = lax.all_to_all(summed.reshape(members, count, width), "band", 0, 0)
    back = back.reshape(planes, GROUPS, count, width).transpose(2, 0, 1, 3)
    return back.reshape(count, planes, columns).astype(jnp.float32)


def solution(mesh):
    return jax.shard_map(
        body,
        mesh=mesh,
        in_specs=(P("band", "space", None), P("space", None), P()),
        out_specs=P("band", "space", None),
        check_vma=False,
    )
```

```python
import functools

import jax
import jax.numpy as jnp
import numpy as np
from jax import lax
from jax.experimental import pallas as pl
from jax.experimental.pallas import tpu as pltpu
from jax.sharding import PartitionSpec as P

NY = 48
NZ = 96
LANE = 128
ROWS = 8
GROUPS = 4
RUNS = NY // GROUPS
ZI = 3
ZB = NZ // ZI
PIECES = RUNS * ZI
ROW_BLOCK = GROUPS * NZ

CENTER = 4.75
HALF_WIDTH = 3.75
NEAR = -2.0 / 3.0 / HALF_WIDTH
FAR = 1.0 / 24.0 / HALF_WIDTH


def lanes_of(rows):
    return lax.broadcasted_iota(jnp.int32, (rows, LANE), 1)


def piece(j):
    return pl.ds(j * LANE, LANE)


def split_groups(four, odd, upper):
    half = {}
    for i in (0, 2):
        half[i] = jnp.where(odd, pltpu.roll(four[i + 1], ZB, 1), four[i])
        half[i + 1] = jnp.where(odd, four[i + 1], pltpu.roll(four[i], LANE - ZB, 1))
    done = {}
    for i in (0, 1):
        done[i] = jnp.where(upper, pltpu.roll(half[i + 2], 2 * ZB, 1), half[i])
        done[i + 2] = jnp.where(upper, half[i + 2], pltpu.roll(half[i], 2 * ZB, 1))
    return done


def rounded(x):
    return x.astype(jnp.bfloat16).astype(jnp.float32)


def pack_halo(planes_at, j, to_above, to_below):
    for to, order in ((to_above, (3, 2, 1, 0)), (to_below, (0, 1, 2, 3))):
        near, next_near, far, farthest = [planes_at(p) for p in order]
        for i, x in enumerate((near, next_near)):
            both = jnp.concatenate([x, x - rounded(x)], axis=0)
            to[0, pl.ds(2 * ROWS * i, 2 * ROWS), piece(j)] = both.astype(jnp.bfloat16)
        both = jnp.concatenate([far, farthest], axis=0)
        to[0, pl.ds(4 * ROWS, 2 * ROWS), piece(j)] = both.astype(jnp.bfloat16)


def unpack_halo(halo, field, order):
    near, next_near, far, farthest = order
    columns = field.shape[2]
    for at in range(0, columns, ROW_BLOCK):
        lanes = pl.ds(at, ROW_BLOCK)
        for i, p in enumerate((near, next_near)):
            both = halo[0, pl.ds(2 * ROWS * i, 2 * ROWS), lanes].astype(jnp.float32)
            field[p, :, lanes] = both[:ROWS] + both[ROWS:]
        both = halo[0, pl.ds(4 * ROWS, 2 * ROWS), lanes].astype(jnp.float32)
        field[far, :, lanes] = both[:ROWS]
        field[farthest, :, lanes] = both[ROWS:]


def halo_shape(count, columns):
    return jax.ShapeDtypeStruct((count // ROWS, 6 * ROWS, columns), jnp.bfloat16)


def halo_spec(columns):
    return pl.BlockSpec((1, 6 * ROWS, columns), lambda i: (i, 0, 0))


def to_runs_kernel(cells, order, out, to_above, to_below, terms, turned):
    planes, rows, columns = out.shape
    blocks = columns // ROW_BLOCK
    for k in range(blocks):
        for pair in range(planes // 2):
            x = cells[2 * pair : 2 * pair + 2, :, pl.ds(k * ROW_BLOCK, ROW_BLOCK)].reshape(2 * rows, ROW_BLOCK)
            at = pl.ds((k * (planes // 2) + pair) * 2 * rows, 2 * rows)
            first = rounded(x)
            second = rounded(x - first)
            terms[0, at] = first.astype(jnp.bfloat16)
            terms[1, at] = second.astype(jnp.bfloat16)
            terms[2, at] = (x - first - second).astype(jnp.bfloat16)
    parts = [jnp.dot(terms[i], order[...], preferred_element_type=jnp.float32) for i in range(3)]
    turned[...] = parts[0] + (parts[1] + parts[2])

    group = lanes_of(rows) // ZB
    odd = group % 2 == 1
    upper = group >= 2
    per_group = blocks // GROUPS
    for m in range(PIECES // GROUPS):
        done = []
        for p in range(planes):
            four = [
                turned[pl.ds((a * per_group + m // ZI) * planes * rows + p * rows, rows), piece(m % ZI)]
                for a in range(GROUPS)
            ]
            done.append(split_groups(four, odd, upper))
        for i in range(GROUPS):
            j = GROUPS * m + i
            for p in range(planes):
                out[p, :, piece(j)] = done[p][i]
            pack_halo(lambda p: done[p][i], j, to_above, to_below)


def to_runs(cells):
    planes, count, columns = cells.shape
    order = z_order().T
    spec = pl.BlockSpec((planes, ROWS, columns), lambda i: (0, i, 0))
    halo = halo_spec(columns)
    total = planes * ROWS * columns // ROW_BLOCK
    return pl.pallas_call(
        to_runs_kernel,
        grid=(count // ROWS,),
        in_specs=[spec, pl.BlockSpec(order.shape, lambda i: (0, 0))],
        out_specs=[spec, halo, halo],
        out_shape=[jax.ShapeDtypeStruct(cells.shape, cells.dtype)] + [halo_shape(count, columns)] * 2,
        scratch_shapes=[
            pltpu.VMEM((3, total, ROW_BLOCK), jnp.bfloat16),
            pltpu.VMEM((total, ROW_BLOCK), jnp.float32),
        ],
        compiler_params=pltpu.CompilerParams(vmem_limit_bytes=32 * 1024 * 1024),
        cost_estimate=pl.CostEstimate(flops=40000 * count * columns, bytes_accessed=cells.size * 8, transcendentals=0),
    )(cells, order)


def stencil_row(src, plane, masks, emit):
    a_last, a_first, zb_last, zb_first = masks
    centers, turned = {}, {}

    def center(b, zi):
        if (b, zi) not in centers:
            centers[b, zi] = src[plane + 2, :, piece(ZI * b + zi)]
        return centers[b, zi]

    def turn(b, zi, by, mask):
        if (b, zi, by) not in turned:
            turned[b, zi, by] = jnp.where(mask, 0.0, pltpu.roll(center(b, zi), by, 1))
        return turned[b, zi, by]

    def at_y(b, zi):
        if b < 0:
            return turn(b + RUNS, zi, ZB, a_first)
        if b >= RUNS:
            return turn(b - RUNS, zi, LANE - ZB, a_last)
        return center(b, zi)

    def at_z(b, zi):
        if zi < 0:
            return turn(b, zi + ZI, 1, zb_first)
        if zi >= ZI:
            return turn(b, zi - ZI, LANE - 1, zb_last)
        return center(b, zi)

    def at_x(j, k):
        return src[plane + 2 + k, :, piece(j)]

    for b in range(RUNS):
        for zi in range(ZI):
            j = ZI * b + zi
            near, far = [
                (at_x(j, -k) + at_x(j, k)) + (at_y(b - k, zi) + at_y(b + k, zi)) + (at_z(b, zi - k) + at_z(b, zi + k))
                for k in (1, 2)
            ]
            emit(j, center(b, zi), near, far)


def two_steps_kernel(last, inside, below, own, above, potential, *rest):
    if last:
        first, out, field, inner, diag = rest
    else:
        out, to_above, to_below, field, inner, diag = rest
    planes, rows, columns = own.shape

    @pl.when(pl.program_id(0) == 0)
    def _():
        for p in range(planes + 4):
            scaled = (potential[p : p + 1, :] + (HALF_WIDTH - CENTER)) / HALF_WIDTH
            diag[p] = jnp.broadcast_to(scaled, (rows, columns))

    unpack_halo(below, field, (3, 2, 1, 0))
    field[planes : 2 * planes] = own[...]
    unpack_halo(above, field, (8, 9, 10, 11))

    lane = lanes_of(rows)
    masks = (lane >= LANE - ZB, lane < ZB, lane % ZB == ZB - 1, lane % ZB == 0)
    odd = lane // ZB % 2 == 1
    upper = lane >= 2 * ZB

    def first_stage(p, _):
        here = jnp.where(p < 2, inside[0], jnp.where(p >= planes + 2, inside[1], 1.0))
        near_by = here * NEAR
        far_by = here * FAR

        def emit(j, center, near, far):
            inner[p, :, piece(j)] = diag[p, :, piece(j)] * center + near_by * near + far_by * far

        stencil_row(field, p + planes - 4, masks, emit)
        return 0

    lax.fori_loop(0, planes + 4, first_stage, 0)

    def second_stage(p, _):
        held = []

        def emit(j, center, near, far):
            total = diag[p + 2, :, piece(j)] * center + NEAR * near + FAR * far
            total = 2.0 * total - field[p + planes, :, piece(j)]
            if not last:
                out[p, :, piece(j)] = total
                return
            held.append(2.0 * total - first[p, :, piece(j)])
            if len(held) == GROUPS:
                done = split_groups(held, odd, upper)
                for a in range(GROUPS):
                    out[GROUPS * p + a, :, piece(j // GROUPS)] = done[a]
                held.clear()

        stencil_row(inner, p, masks, emit)
        return 0

    lax.fori_loop(0, planes, second_stage, 0)
    if not last:
        for j in range(PIECES):
            pack_halo(lambda p: out[p, :, piece(j)], j, to_above, to_below)


def two_steps(inside, below, own, above, potential, first=None):
    planes, count, columns = own.shape
    last = first is not None
    spec = pl.BlockSpec((planes, ROWS, columns), lambda i: (0, i, 0))
    halo = halo_spec(columns)
    out_shape = [jax.ShapeDtypeStruct(own.shape, own.dtype)] + [halo_shape(count, columns)] * 2
    out_spec = [spec, halo, halo]
    if last:
        width = columns // GROUPS
        out_shape = jax.ShapeDtypeStruct((planes * GROUPS, count, width), jnp.float32)
        out_spec = pl.BlockSpec((planes * GROUPS, ROWS, width), lambda i: (0, i, 0))
    return pl.pallas_call(
        functools.partial(two_steps_kernel, last),
        grid=(count // ROWS,),
        in_specs=[
            pl.BlockSpec(memory_space=pltpu.SMEM),
            halo,
            spec,
            halo,
            pl.BlockSpec(potential.shape, lambda i: (0, 0)),
        ]
        + [spec] * last,
        out_specs=out_spec,
        out_shape=out_shape,
        scratch_shapes=[
            pltpu.VMEM((planes * 3, ROWS, columns), jnp.float32),
            pltpu.VMEM((planes + 4, ROWS, columns), jnp.float32),
            pltpu.VMEM((planes + 4, ROWS, columns), jnp.float32),
        ],
        compiler_params=pltpu.CompilerParams(vmem_limit_bytes=32 * 1024 * 1024),
        cost_estimate=pl.CostEstimate(flops=80000 * count * columns, bytes_accessed=own.size * 16, transcendentals=0),
    )(inside, below, own, above, potential, *([first] if last else []))


def z_order():
    one = np.zeros((NZ, NZ), np.float32)
    for z in range(NZ):
        one[z % ZI * ZB + z // ZI, z] = 1.0
    return jnp.asarray(np.kron(np.eye(GROUPS, dtype=np.float32), one), jnp.bfloat16)


def rotate_kernel(weights, cells, order, out):
    for k in range(cells.shape[1] // ROW_BLOCK):
        at = pl.ds(k * ROW_BLOCK, ROW_BLOCK)
        summed = jnp.dot(weights[...], cells[:, at], preferred_element_type=jnp.float32).astype(jnp.bfloat16)
        out[:, at] = jnp.dot(summed, order[...], preferred_element_type=jnp.float32).astype(jnp.bfloat16)


def rotate(weights, cells):
    return pl.pallas_call(
        rotate_kernel,
        out_shape=jax.ShapeDtypeStruct((weights.shape[0], cells.shape[1]), jnp.bfloat16),
        compiler_params=pltpu.CompilerParams(vmem_limit_bytes=32 * 1024 * 1024),
        cost_estimate=pl.CostEstimate(
            flops=4 * weights.size * cells.shape[1], bytes_accessed=4 * cells.size, transcendentals=0
        ),
    )(weights, cells, z_order())


def body(orbitals, potential, rotation):
    count, planes, columns = orbitals.shape
    domains = lax.axis_size("space")
    members = lax.axis_size("band")
    up = [(i, i + 1) for i in range(domains - 1)]
    down = [(i + 1, i) for i in range(domains - 1)]

    def around(to_above, to_below):
        return lax.ppermute(to_above, "space", up), lax.ppermute(to_below, "space", down)

    at = lax.axis_index("space")
    inside = jnp.stack([at > 0, at < domains - 1]).astype(jnp.float32)

    zeroth, *halo = to_runs(orbitals.transpose(1, 0, 2))
    below, above = around(*halo)

    runs = potential.reshape(planes, GROUPS, RUNS, ZB, ZI).transpose(0, 2, 4, 1, 3).reshape(planes, columns)
    potential_below = lax.ppermute(runs[planes - 2 :], "space", up)
    potential_above = lax.ppermute(runs[:2], "space", down)
    field = jnp.concatenate([potential_below, runs, potential_above], axis=0)

    second, *halo = two_steps(inside, below, zeroth, above, field)
    below, above = around(*halo)
    filtered = two_steps(inside, below, second, above, field, first=zeroth).astype(jnp.bfloat16)
    gathered = lax.all_to_all(filtered, "band", 0, 0)
    width = columns // GROUPS
    summed = rotate(rotation.T, gathered.reshape(members * count, width))
    back = lax.all_to_all(summed.reshape(members, count, width), "band", 0, 0)
    back = back.reshape(planes, GROUPS, count, width).transpose(2, 0, 1, 3)
    return back.reshape(count, planes, columns).astype(jnp.float32)


def solution(mesh):
    return jax.shard_map(
        body,
        mesh=mesh,
        in_specs=(P("band", "space", None), P("space", None), P()),
        out_specs=P("band", "space", None),
        check_vma=False,
    )
```

```python
import functools

import jax
import jax.numpy as jnp
import numpy as np
from jax import lax
from jax.experimental import pallas as pl
from jax.experimental.pallas import tpu as pltpu
from jax.sharding import PartitionSpec as P

NY = 48
NZ = 96
LANE = 128
ROWS = 8
GROUPS = 4
RUNS = NY // GROUPS
ZI = 3
ZB = NZ // ZI
PIECES = RUNS * ZI
ROW_BLOCK = GROUPS * NZ
VMEM_LIMIT = 18 * 1024 * 1024
CHUNKS = (16, 8)

CENTER = 4.75
HALF_WIDTH = 3.75
NEAR = -2.0 / 3.0 / HALF_WIDTH
FAR = 1.0 / 24.0 / HALF_WIDTH


def lanes_of(rows):
    return lax.broadcasted_iota(jnp.int32, (rows, LANE), 1)


def piece(j):
    return pl.ds(j * LANE, LANE)


def split_groups(four, odd, upper):
    half = {}
    for i in (0, 2):
        half[i] = jnp.where(odd, pltpu.roll(four[i + 1], ZB, 1), four[i])
        half[i + 1] = jnp.where(odd, four[i + 1], pltpu.roll(four[i], LANE - ZB, 1))
    done = {}
    for i in (0, 1):
        done[i] = jnp.where(upper, pltpu.roll(half[i + 2], 2 * ZB, 1), half[i])
        done[i + 2] = jnp.where(upper, half[i + 2], pltpu.roll(half[i], 2 * ZB, 1))
    return done


def rounded(x):
    return x.astype(jnp.bfloat16).astype(jnp.float32)


def pack_halo(planes, odd, to_mate, to_other):
    base = pl.program_id(0) * 3
    for to, upward in ((to_mate, 1 - odd), (to_other, odd)):
        near, next_near, far, farthest = [jnp.where(upward == 1, 3 - k, k) for k in range(4)]
        for j in range(PIECES):
            for i, p in enumerate((near, next_near)):
                x = planes[p, :, piece(j)]
                to[base + i, :, piece(j)] = jnp.concatenate([x, x - rounded(x)], axis=0).astype(jnp.bfloat16)
            both = jnp.concatenate([planes[far, :, piece(j)], planes[farthest, :, piece(j)]], axis=0)
            to[base + 2, :, piece(j)] = both.astype(jnp.bfloat16)


def unpack_halo(halo, below, field):
    base = pl.program_id(0) * 3
    near, next_near, far, farthest = [jnp.where(below == 1, 3 - k, 8 + k) for k in range(4)]
    columns = field.shape[2]
    for at in range(0, columns, ROW_BLOCK):
        lanes = pl.ds(at, ROW_BLOCK)
        for i, p in enumerate((near, next_near)):
            both = halo[base + i, :, lanes].astype(jnp.float32)
            field[p, :, lanes] = both[:ROWS] + both[ROWS:]
        both = halo[base + 2, :, lanes].astype(jnp.float32)
        field[far, :, lanes] = both[:ROWS]
        field[farthest, :, lanes] = both[ROWS:]


def halo_shape(count, columns, extra=0):
    return jax.ShapeDtypeStruct((count // ROWS * 3 + extra, 2 * ROWS, columns), jnp.bfloat16)


def whole_spec(shape):
    return pl.BlockSpec(shape, lambda i: (0,) * len(shape))


def split_terms(x, terms, at):
    first = rounded(x)
    second = rounded(x - first)
    terms[0, at] = first.astype(jnp.bfloat16)
    terms[1, at] = second.astype(jnp.bfloat16)
    terms[2, at] = (x - first - second).astype(jnp.bfloat16)


def reordered(terms, order):
    parts = [jnp.dot(terms[i], order[...], preferred_element_type=jnp.float32) for i in range(3)]
    return parts[0] + (parts[1] + parts[2])


def potential_to_runs(cells, odd, order, out, to_mate, to_other, gathered, terms):
    planes, columns = cells.shape
    blocks = columns // ROW_BLOCK
    at_row = lax.broadcasted_iota(jnp.int32, (ROWS, LANE), 0)
    for k in range(blocks):
        x = cells[:, pl.ds(k * ROW_BLOCK, ROW_BLOCK)]
        gathered[pl.ds(k * ROWS, ROWS), :] = jnp.concatenate([x, jnp.zeros_like(x)], axis=0)
    split_terms(gathered[...], terms, pl.ds(0, blocks * ROWS))
    gathered[...] = reordered(terms, order)
    group = lanes_of(ROWS) // ZB
    per_group = blocks // GROUPS
    for m in range(PIECES // GROUPS):
        four = [gathered[pl.ds((a * per_group + m // ZI) * ROWS, ROWS), piece(m % ZI)] for a in range(GROUPS)]
        done = split_groups(four, group % 2 == 1, group >= 2)
        for i in range(GROUPS):
            x = done[i]
            j = GROUPS * m + i
            out[:, piece(j)] = x[:planes]
            for to, upward in ((to_mate, 1 - odd), (to_other, odd)):
                near = jnp.where(upward == 1, x[planes - 1 : planes], x[0:1])
                next_near = jnp.where(upward == 1, x[planes - 2 : planes - 1], x[1:2])
                rows = [near, near - rounded(near), next_near, next_near - rounded(next_near)]
                total = jnp.zeros((ROWS, LANE), jnp.float32)
                for r, row in enumerate(rows):
                    total = jnp.where(at_row == r, row, total)
                total = jnp.concatenate([total, jnp.zeros_like(total)], axis=0)
                to[to.shape[0] - 1, :, piece(j)] = total.astype(jnp.bfloat16)


def to_runs_kernel(extra, place, cells, *rest):
    if extra:
        potential, out, to_mate, to_other, runs, order, terms, turned, gathered, few_terms = rest
    else:
        out, to_mate, to_other, order, terms, turned = rest
    planes, rows, columns = out.shape
    blocks = columns // ROW_BLOCK

    @pl.when(pl.program_id(0) == 0)
    def _():
        to = lax.broadcasted_iota(jnp.int32, order.shape, 1)
        source = to // NZ * NZ + to % ZB * ZI + to % NZ // ZB
        order[...] = jnp.where(lax.broadcasted_iota(jnp.int32, order.shape, 0) == source, 1.0, 0.0).astype(jnp.bfloat16)
        if extra:
            potential_to_runs(potential, place[2], order, runs, to_mate, to_other, gathered, few_terms)

    for k in range(blocks):
        x = cells[:, :, pl.ds(k * ROW_BLOCK, ROW_BLOCK)].reshape(rows * planes, ROW_BLOCK)
        split_terms(x, terms, pl.ds(k * rows * planes, rows * planes))
    whole = reordered(terms, order)
    for zi in range(ZI):
        turned[zi] = whole[:, zi * LANE : (zi + 1) * LANE]

    group = lanes_of(rows) // ZB
    odd = group % 2 == 1
    upper = group >= 2
    per_group = blocks // GROUPS
    for m in range(PIECES // GROUPS):
        for p in range(planes):
            four = []
            for a in range(GROUPS):
                k = a * per_group + m // ZI
                four.append(turned[m % ZI, pl.ds(k * rows * planes + p, rows, stride=planes), :])
            done = split_groups(four, odd, upper)
            for i in range(GROUPS):
                out[p, :, piece(GROUPS * m + i)] = done[i]
    pack_halo(out, place[2], to_mate, to_other)


def to_runs(place, cells, start, count, potential=None):
    _, planes, columns = cells.shape
    extra = potential is not None
    halo = halo_shape(count, columns, int(extra))
    blocks = columns // ROW_BLOCK
    total = planes * ROWS * blocks
    scratch = [
        pltpu.VMEM((ROW_BLOCK, ROW_BLOCK), jnp.bfloat16),
        pltpu.VMEM((3, total, ROW_BLOCK), jnp.bfloat16),
        pltpu.VMEM((ZI, total, LANE), jnp.float32),
    ]
    if extra:
        scratch.append(pltpu.VMEM((blocks * ROWS, ROW_BLOCK), jnp.float32))
        scratch.append(pltpu.VMEM((3, blocks * ROWS, ROW_BLOCK), jnp.bfloat16))
    return pl.pallas_call(
        functools.partial(to_runs_kernel, extra),
        grid=(count // ROWS,),
        in_specs=[
            pl.BlockSpec(memory_space=pltpu.SMEM),
            pl.BlockSpec((ROWS, planes, columns), lambda i: (start // ROWS + i, 0, 0)),
        ]
        + [whole_spec((planes, columns))] * extra,
        out_specs=[pl.BlockSpec((planes, ROWS, columns), lambda i: (0, i, 0))]
        + [whole_spec(halo.shape)] * 2
        + [whole_spec((planes, columns))] * extra,
        out_shape=[pltpu.HBM((planes, count, columns), cells.dtype), halo, halo]
        + [jax.ShapeDtypeStruct((planes, columns), jnp.float32)] * extra,
        scratch_shapes=scratch,
        compiler_params=pltpu.CompilerParams(vmem_limit_bytes=VMEM_LIMIT),
        cost_estimate=pl.CostEstimate(flops=1, bytes_accessed=1, transcendentals=0),
    )(place, cells, *([potential] if extra else []))


def stencil_row(src, plane, masks, emit):
    a_last, a_first, zb_last, zb_first = masks
    centers, turned = {}, {}

    def center(b, zi):
        if (b, zi) not in centers:
            centers[b, zi] = src[plane + 2, :, piece(ZI * b + zi)]
        return centers[b, zi]

    def turn(b, zi, by, mask):
        if (b, zi, by) not in turned:
            turned[b, zi, by] = jnp.where(mask, 0.0, pltpu.roll(center(b, zi), by, 1))
        return turned[b, zi, by]

    def at_y(b, zi):
        if b < 0:
            return turn(b + RUNS, zi, ZB, a_first)
        if b >= RUNS:
            return turn(b - RUNS, zi, LANE - ZB, a_last)
        return center(b, zi)

    def at_z(b, zi):
        if zi < 0:
            return turn(b, zi + ZI, 1, zb_first)
        if zi >= ZI:
            return turn(b, zi - ZI, LANE - 1, zb_last)
        return center(b, zi)

    def at_x(j, k):
        return src[plane + 2 + k, :, piece(j)]

    for b in range(RUNS):
        for zi in range(ZI):
            j = ZI * b + zi
            near, far = [
                (at_x(j, -k) + at_x(j, k)) + (at_y(b - k, zi) + at_y(b + k, zi)) + (at_z(b, zi - k) + at_z(b, zi + k))
                for k in (1, 2)
            ]
            emit(j, center(b, zi), near, far)


def potential_field_kernel(place, from_mate, own, from_other, out):
    planes = own.shape[0]

    def scale(x):
        return (x + (HALF_WIDTH - CENTER)) / HALF_WIDTH

    out[2 : planes + 2] = scale(own[...])
    mate, other = [halo[0].astype(jnp.float32) for halo in (from_mate, from_other)]
    mate_below = place[2] == 1
    below = jnp.where(mate_below, mate, other)
    above = jnp.where(mate_below, other, mate)
    out[1:2] = scale(below[0:1] + below[1:2])
    out[0:1] = scale(below[2:3] + below[3:4])
    out[planes + 2 : planes + 3] = scale(above[0:1] + above[1:2])
    out[planes + 3 : planes + 4] = scale(above[2:3] + above[3:4])


def potential_field(place, halo, own):
    planes, columns = own.shape
    specs = [pl.BlockSpec((1,) + x.shape[1:], lambda i, n=x.shape[0]: (n - 1, 0, 0)) for x in halo]
    return pl.pallas_call(
        potential_field_kernel,
        grid=(1,),
        in_specs=[pl.BlockSpec(memory_space=pltpu.SMEM), specs[0], whole_spec(own.shape), specs[1]],
        out_specs=whole_spec((planes + 4, columns)),
        out_shape=jax.ShapeDtypeStruct((planes + 4, columns), jnp.float32),
        compiler_params=pltpu.CompilerParams(vmem_limit_bytes=VMEM_LIMIT),
    )(place, halo[0], own, halo[1])


def two_steps_kernel(last, count_done, *refs):
    done = refs[:count_done]
    place, from_mate, own, from_other, potential, *rest = refs[count_done:]
    if last:
        first, out, field, inner, diag, held_all = rest
    else:
        out, to_mate, to_other, field, inner, diag = rest
    planes, rows, columns = own.shape

    @pl.when(pl.program_id(0) == 0)
    def _():
        for p in range(planes + 4):
            diag[p] = jnp.broadcast_to(potential[p : p + 1, :], (rows, columns))

    unpack_halo(from_mate, place[2], field)
    field[planes : 2 * planes] = own[...]
    unpack_halo(from_other, 1 - place[2], field)

    lane = lanes_of(rows)
    masks = (lane >= LANE - ZB, lane < ZB, lane % ZB == ZB - 1, lane % ZB == 0)
    odd = lane // ZB % 2 == 1
    upper = lane >= 2 * ZB

    def first_stage(p, _):
        here = jnp.where(p < 2, place[0], jnp.where(p >= planes + 2, place[1], 1)).astype(jnp.float32)
        near_by = here * NEAR
        far_by = here * FAR

        def emit(j, center, near, far):
            inner[p, :, piece(j)] = diag[p, :, piece(j)] * center + near_by * near + far_by * far

        stencil_row(field, p + planes - 4, masks, emit)
        return 0

    lax.fori_loop(0, planes + 4, first_stage, 0)

    own_rows = pl.ds(pl.multiple_of(pl.program_id(0) * rows, rows), rows)

    def second_stage(p, _):
        held = []

        def emit(j, center, near, far):
            total = diag[p + 2, :, piece(j)] * center + NEAR * near + FAR * far
            total = 2.0 * total - field[p + planes, :, piece(j)]
            if not last:
                out[p, :, piece(j)] = total
                return
            held.append(2.0 * total - first[p, :, piece(j)])
            if len(held) == GROUPS:
                done = split_groups(held, odd, upper)
                for a in range(GROUPS):
                    held_all[GROUPS * p + a, own_rows, piece(j // GROUPS)] = done[a]
                held.clear()

        stencil_row(inner, p, masks, emit)
        return 0

    lax.fori_loop(0, planes, second_stage, 0)
    if not last:
        pack_halo(out, place[2], to_mate, to_other)
        return

    @pl.when(pl.program_id(0) == pl.num_programs(0) - 1)
    def _():
        def one_part(i, _):
            both = [x[i].astype(jnp.float32) for x in done] + [held_all[i]]
            out[i] = jnp.concatenate(both, axis=0).astype(jnp.bfloat16)
            return 0

        lax.fori_loop(0, out.shape[0], one_part, 0)


def two_steps(place, halo, own, potential, first=None, done=()):
    planes, count, columns = own.shape
    last = first is not None
    spec = pl.BlockSpec((planes, ROWS, columns), lambda i: (0, i, 0))
    near = halo_shape(count, columns)
    out_shape = [jax.ShapeDtypeStruct(own.shape, own.dtype), near, near]
    out_spec = [spec, whole_spec(near.shape), whole_spec(near.shape)]
    scratch = [
        pltpu.VMEM((planes * 3, ROWS, columns), jnp.float32),
        pltpu.VMEM((planes + 4, ROWS, columns), jnp.float32),
        pltpu.VMEM((planes + 4, ROWS, columns), jnp.float32),
    ]
    if last:
        shape = (planes * GROUPS, count, columns // GROUPS)
        scratch.append(pltpu.VMEM(shape, jnp.float32))
        shape = (planes * GROUPS, count + sum(x.shape[1] for x in done), columns // GROUPS)
        out_shape = jax.ShapeDtypeStruct(shape, jnp.bfloat16)
        out_spec = pl.BlockSpec(shape, lambda i: (0, 0, 0))
    return pl.pallas_call(
        functools.partial(two_steps_kernel, last, len(done)),
        grid=(count // ROWS,),
        in_specs=[whole_spec(x.shape) for x in done]
        + [pl.BlockSpec(memory_space=pltpu.SMEM)]
        + [whole_spec(halo[0].shape), spec, whole_spec(halo[1].shape), whole_spec(potential.shape)]
        + [spec] * last,
        out_specs=out_spec,
        out_shape=out_shape,
        scratch_shapes=scratch,
        compiler_params=pltpu.CompilerParams(vmem_limit_bytes=VMEM_LIMIT),
        cost_estimate=pl.CostEstimate(flops=1, bytes_accessed=1, transcendentals=0),
    )(*done, place, halo[0], own, halo[1], potential, *([first] if last else []))


def z_order():
    one = np.zeros((NZ, NZ), np.float32)
    for z in range(NZ):
        one[z % ZI * ZB + z // ZI, z] = 1.0
    return jnp.asarray(np.kron(np.eye(GROUPS, dtype=np.float32), one), jnp.bfloat16)


def rotate_kernel(weights, cells, order, out):
    for k in range(cells.shape[1] // ROW_BLOCK):
        at = pl.ds(k * ROW_BLOCK, ROW_BLOCK)
        summed = jnp.dot(weights[...], cells[:, at], preferred_element_type=jnp.float32).astype(jnp.bfloat16)
        out[:, at] = jnp.dot(summed, order[...], preferred_element_type=jnp.float32).astype(jnp.bfloat16)


def rotate(weights, cells):
    return pl.pallas_call(
        rotate_kernel,
        out_shape=jax.ShapeDtypeStruct((weights.shape[0], cells.shape[1]), jnp.bfloat16),
        compiler_params=pltpu.CompilerParams(vmem_limit_bytes=VMEM_LIMIT),
        cost_estimate=pl.CostEstimate(flops=1, bytes_accessed=1, transcendentals=0),
    )(weights, cells, z_order())


def from_parts_kernel(parts, out, mixed):
    rows, planes, columns = out.shape
    width = parts.shape[2]
    groups = columns // width
    for p in range(planes):
        for a in range(groups):
            x = parts[p * groups + a].astype(jnp.float32)
            for j in range(width // LANE):
                for o in range(0, rows, ROWS):
                    at = pl.ds(o * planes + p, ROWS, stride=planes)
                    mixed[a * (width // LANE) + j, at, :] = x[o : o + ROWS, j * LANE : (j + 1) * LANE]
    for j in range(columns // LANE):
        out[:, :, piece(j)] = mixed[j].reshape(rows, planes, LANE)


def from_parts(parts, planes):
    n, count, width = parts.shape
    columns = n // planes * width
    return pl.pallas_call(
        from_parts_kernel,
        grid=(1,),
        in_specs=[pl.BlockSpec(parts.shape, lambda i: (0, 0, 0))],
        out_specs=pl.BlockSpec((count, planes, columns), lambda i: (0, 0, 0)),
        out_shape=jax.ShapeDtypeStruct((count, planes, columns), jnp.float32),
        scratch_shapes=[pltpu.VMEM((columns // LANE, count * planes, LANE), jnp.float32)],
        compiler_params=pltpu.CompilerParams(vmem_limit_bytes=VMEM_LIMIT),
        cost_estimate=pl.CostEstimate(flops=1, bytes_accessed=1, transcendentals=0),
    )(parts)


def body(orbitals, potential, rotation):
    count, planes, columns = orbitals.shape
    domains = lax.axis_size("space")
    members = lax.axis_size("band")
    mates = [(i, i ^ 1) for i in range(domains)]
    others = [(i, i + 1) for i in range(1, domains - 1, 2)]
    others = others + [(j, i) for i, j in others]

    def around(to_mate, to_other):
        other = lax.ppermute(to_other, "space", others)
        return lax.ppermute(to_mate, "space", mates), other

    at = lax.axis_index("space")
    place = jnp.stack([at > 0, at < domains - 1, at % 2]).astype(jnp.int32)

    orbitals = pltpu.with_memory_space_constraint(orbitals, pltpu.HBM)
    starts = [sum(CHUNKS[:i]) for i in range(len(CHUNKS))]
    zeroth, halos = [], []
    for i, (start, chunk) in enumerate(zip(starts, CHUNKS)):
        fields, *halo = to_runs(place, orbitals, start, chunk, potential if i == 0 else None)
        if i == 0:
            field = halo.pop()
        zeroth.append(fields)
        halos.append(around(*halo))

    second, next_halos = [], []
    fields_0, waited = lax.optimization_barrier((zeroth[0], halos[1][0]))
    halos[1] = (waited, halos[1][1])
    field = potential_field(place, halos[0], field)
    fields, *halo = two_steps(place, halos[0], fields_0, field)
    second.append(fields)
    next_halos.append(around(*halo))
    fields_1 = zeroth[1]
    fields, *halo = two_steps(place, halos[1], fields_1, field)
    second.append(fields)
    next_halos.append(around(*halo))
    filtered = ()
    for fields, halo, first in zip(second, next_halos, zeroth):
        filtered = (two_steps(place, halo, fields, field, first, filtered),)
    filtered, = filtered
    gathered = lax.all_to_all(filtered, "band", 0, 0)
    width = columns // GROUPS
    summed = rotate(rotation.T, gathered.reshape(members * count, width))
    back = lax.all_to_all(summed.reshape(members, count, width), "band", 0, 0)
    return from_parts(back, planes)


def solution(mesh):
    return jax.shard_map(
        body,
        mesh=mesh,
        in_specs=(P("band", "space", None), P("space", None), P()),
        out_specs=P("band", "space", None),
        check_vma=False,
    )
```

```python
import functools

import jax
import jax.numpy as jnp
import numpy as np
from jax import lax
from jax.experimental import pallas as pl
from jax.experimental.pallas import tpu as pltpu
from jax.sharding import PartitionSpec as P

NY = 48
NZ = 96
LANE = 128
ROWS = 8
GROUPS = 4
RUNS = NY // GROUPS
ZI = 3
ZB = NZ // ZI
PIECES = RUNS * ZI
ROW_BLOCK = GROUPS * NZ
VMEM_LIMIT = 18 * 1024 * 1024
CHUNKS = (16, 8)

CENTER = 4.75
HALF_WIDTH = 3.75
NEAR = -2.0 / 3.0 / HALF_WIDTH
FAR = 1.0 / 24.0 / HALF_WIDTH


def lanes_of(rows):
    return lax.broadcasted_iota(jnp.int32, (rows, LANE), 1)


def piece(j):
    return pl.ds(j * LANE, LANE)


def split_groups(four, odd, upper):
    half = {}
    for i in (0, 2):
        half[i] = jnp.where(odd, pltpu.roll(four[i + 1], ZB, 1), four[i])
        half[i + 1] = jnp.where(odd, four[i + 1], pltpu.roll(four[i], LANE - ZB, 1))
    done = {}
    for i in (0, 1):
        done[i] = jnp.where(upper, pltpu.roll(half[i + 2], 2 * ZB, 1), half[i])
        done[i + 2] = jnp.where(upper, half[i + 2], pltpu.roll(half[i], 2 * ZB, 1))
    return done


def rounded(x):
    return x.astype(jnp.bfloat16).astype(jnp.float32)


def pack_halo(planes, odd, to_mate, to_other):
    base = pl.program_id(0) * 3
    for to, upward in ((to_mate, 1 - odd), (to_other, odd)):
        near, next_near, far, farthest = [jnp.where(upward == 1, 3 - k, k) for k in range(4)]
        for j in range(PIECES):
            for i, p in enumerate((near, next_near)):
                x = planes[p, :, piece(j)]
                to[base + i, :, piece(j)] = jnp.concatenate([x, x - rounded(x)], axis=0).astype(jnp.bfloat16)
            both = jnp.concatenate([planes[far, :, piece(j)], planes[farthest, :, piece(j)]], axis=0)
            to[base + 2, :, piece(j)] = both.astype(jnp.bfloat16)


def unpack_halo(halo, below, field):
    base = pl.program_id(0) * 3
    near, next_near, far, farthest = [jnp.where(below == 1, 3 - k, 8 + k) for k in range(4)]
    columns = field.shape[2]
    for at in range(0, columns, ROW_BLOCK):
        lanes = pl.ds(at, ROW_BLOCK)
        for i, p in enumerate((near, next_near)):
            both = halo[base + i, :, lanes].astype(jnp.float32)
            field[p, :, lanes] = both[:ROWS] + both[ROWS:]
        both = halo[base + 2, :, lanes].astype(jnp.float32)
        field[far, :, lanes] = both[:ROWS]
        field[farthest, :, lanes] = both[ROWS:]


def halo_shape(count, columns, extra=0):
    return jax.ShapeDtypeStruct((count // ROWS * 3 + extra, 2 * ROWS, columns), jnp.bfloat16)


def whole_spec(shape):
    return pl.BlockSpec(shape, lambda i: (0,) * len(shape))


def split_terms(x, terms, at):
    first = rounded(x)
    second = rounded(x - first)
    terms[0, at] = first.astype(jnp.bfloat16)
    terms[1, at] = second.astype(jnp.bfloat16)
    terms[2, at] = (x - first - second).astype(jnp.bfloat16)


def reordered(terms, order):
    parts = [jnp.dot(terms[i], order[...], preferred_element_type=jnp.float32) for i in range(3)]
    return parts[0] + (parts[1] + parts[2])


def potential_to_runs(cells, odd, order, out, to_mate, to_other, gathered, terms):
    planes, columns = cells.shape
    blocks = columns // ROW_BLOCK
    at_row = lax.broadcasted_iota(jnp.int32, (ROWS, LANE), 0)
    for k in range(blocks):
        x = cells[:, pl.ds(k * ROW_BLOCK, ROW_BLOCK)]
        gathered[pl.ds(k * ROWS, ROWS), :] = jnp.concatenate([x, jnp.zeros_like(x)], axis=0)
    split_terms(gathered[...], terms, pl.ds(0, blocks * ROWS))
    gathered[...] = reordered(terms, order)
    group = lanes_of(ROWS) // ZB
    per_group = blocks // GROUPS
    for m in range(PIECES // GROUPS):
        four = [gathered[pl.ds((a * per_group + m // ZI) * ROWS, ROWS), piece(m % ZI)] for a in range(GROUPS)]
        done = split_groups(four, group % 2 == 1, group >= 2)
        for i in range(GROUPS):
            x = done[i]
            j = GROUPS * m + i
            out[:, piece(j)] = x[:planes]
            for to, upward in ((to_mate, 1 - odd), (to_other, odd)):
                near = jnp.where(upward == 1, x[planes - 1 : planes], x[0:1])
                next_near = jnp.where(upward == 1, x[planes - 2 : planes - 1], x[1:2])
                rows = [near, near - rounded(near), next_near, next_near - rounded(next_near)]
                total = jnp.zeros((ROWS, LANE), jnp.float32)
                for r, row in enumerate(rows):
                    total = jnp.where(at_row == r, row, total)
                total = jnp.concatenate([total, jnp.zeros_like(total)], axis=0)
                to[to.shape[0] - 1, :, piece(j)] = total.astype(jnp.bfloat16)


def to_runs_kernel(extra, place, cells, *rest):
    if extra:
        potential, out, to_mate, to_other, runs, order, terms, turned, gathered, few_terms = rest
    else:
        out, to_mate, to_other, order, terms, turned = rest
    planes, rows, columns = out.shape
    blocks = columns // ROW_BLOCK

    @pl.when(pl.program_id(0) == 0)
    def _():
        to = lax.broadcasted_iota(jnp.int32, order.shape, 1)
        source = to // NZ * NZ + to % ZB * ZI + to % NZ // ZB
        order[...] = jnp.where(lax.broadcasted_iota(jnp.int32, order.shape, 0) == source, 1.0, 0.0).astype(jnp.bfloat16)
        if extra:
            potential_to_runs(potential, place[2], order, runs, to_mate, to_other, gathered, few_terms)

    for k in range(blocks):
        x = cells[:, :, pl.ds(k * ROW_BLOCK, ROW_BLOCK)].reshape(rows * planes, ROW_BLOCK)
        split_terms(x, terms, pl.ds(k * rows * planes, rows * planes))
    whole = reordered(terms, order)
    for zi in range(ZI):
        turned[zi] = whole[:, zi * LANE : (zi + 1) * LANE]

    group = lanes_of(rows) // ZB
    odd = group % 2 == 1
    upper = group >= 2
    per_group = blocks // GROUPS
    for m in range(PIECES // GROUPS):
        for p in range(planes):
            four = []
            for a in range(GROUPS):
                k = a * per_group + m // ZI
                four.append(turned[m % ZI, pl.ds(k * rows * planes + p, rows, stride=planes), :])
            done = split_groups(four, odd, upper)
            for i in range(GROUPS):
                out[p, :, piece(GROUPS * m + i)] = done[i]
    pack_halo(out, place[2], to_mate, to_other)


def to_runs(place, cells, start, count, potential=None):
    _, planes, columns = cells.shape
    extra = potential is not None
    halo = halo_shape(count, columns, int(extra))
    blocks = columns // ROW_BLOCK
    total = planes * ROWS * blocks
    scratch = [
        pltpu.VMEM((ROW_BLOCK, ROW_BLOCK), jnp.bfloat16),
        pltpu.VMEM((3, total, ROW_BLOCK), jnp.bfloat16),
        pltpu.VMEM((ZI, total, LANE), jnp.float32),
    ]
    if extra:
        scratch.append(pltpu.VMEM((blocks * ROWS, ROW_BLOCK), jnp.float32))
        scratch.append(pltpu.VMEM((3, blocks * ROWS, ROW_BLOCK), jnp.bfloat16))
    return pl.pallas_call(
        functools.partial(to_runs_kernel, extra),
        grid=(count // ROWS,),
        in_specs=[
            pl.BlockSpec(memory_space=pltpu.SMEM),
            pl.BlockSpec((ROWS, planes, columns), lambda i: (start // ROWS + i, 0, 0)),
        ]
        + [whole_spec((planes, columns))] * extra,
        out_specs=[pl.BlockSpec((planes, ROWS, columns), lambda i: (0, i, 0))]
        + [whole_spec(halo.shape)] * 2
        + [whole_spec((planes, columns))] * extra,
        out_shape=[pltpu.HBM((planes, count, columns), cells.dtype), halo, halo]
        + [jax.ShapeDtypeStruct((planes, columns), jnp.float32)] * extra,
        scratch_shapes=scratch,
        compiler_params=pltpu.CompilerParams(vmem_limit_bytes=VMEM_LIMIT),
        cost_estimate=pl.CostEstimate(flops=1, bytes_accessed=1, transcendentals=0),
    )(place, cells, *([potential] if extra else []))


def stencil_row(src, plane, masks, emit):
    a_last, a_first, zb_last, zb_first = masks
    centers, turned = {}, {}

    def center(b, zi):
        if (b, zi) not in centers:
            centers[b, zi] = src[plane + 2, :, piece(ZI * b + zi)]
        return centers[b, zi]

    def turn(b, zi, by, mask):
        if (b, zi, by) not in turned:
            turned[b, zi, by] = jnp.where(mask, 0.0, pltpu.roll(center(b, zi), by, 1))
        return turned[b, zi, by]

    def at_y(b, zi):
        if b < 0:
            return turn(b + RUNS, zi, ZB, a_first)
        if b >= RUNS:
            return turn(b - RUNS, zi, LANE - ZB, a_last)
        return center(b, zi)

    def at_z(b, zi):
        if zi < 0:
            return turn(b, zi + ZI, 1, zb_first)
        if zi >= ZI:
            return turn(b, zi - ZI, LANE - 1, zb_last)
        return center(b, zi)

    def at_x(j, k):
        return src[plane + 2 + k, :, piece(j)]

    for b in range(RUNS):
        for zi in range(ZI):
            j = ZI * b + zi
            near, far = [
                (at_x(j, -k) + at_x(j, k)) + (at_y(b - k, zi) + at_y(b + k, zi)) + (at_z(b, zi - k) + at_z(b, zi + k))
                for k in (1, 2)
            ]
            emit(j, center(b, zi), near, far)


def potential_field_kernel(place, from_mate, own, from_other, out):
    planes = own.shape[0]
    scale = scaled_potential
    out[2 : planes + 2] = scale(own[...])
    mate, other = [halo[0].astype(jnp.float32) for halo in (from_mate, from_other)]
    mate_below = place[2] == 1
    below = jnp.where(mate_below, mate, other)
    above = jnp.where(mate_below, other, mate)
    out[1:2] = scale(below[0:1] + below[1:2])
    out[0:1] = scale(below[2:3] + below[3:4])
    out[planes + 2 : planes + 3] = scale(above[0:1] + above[1:2])
    out[planes + 3 : planes + 4] = scale(above[2:3] + above[3:4])


def potential_field(place, halo, own):
    planes, columns = own.shape
    specs = [pl.BlockSpec((1,) + x.shape[1:], lambda i, n=x.shape[0]: (n - 1, 0, 0)) for x in halo]
    return pl.pallas_call(
        potential_field_kernel,
        grid=(1,),
        in_specs=[pl.BlockSpec(memory_space=pltpu.SMEM), specs[0], whole_spec(own.shape), specs[1]],
        out_specs=whole_spec((planes + 4, columns)),
        out_shape=jax.ShapeDtypeStruct((planes + 4, columns), jnp.float32),
        compiler_params=pltpu.CompilerParams(vmem_limit_bytes=VMEM_LIMIT),
    )(place, halo[0], own, halo[1])


def scaled_potential(x):
    return (x + (HALF_WIDTH - CENTER)) / HALF_WIDTH


def shift_masks(rows):
    lane = lanes_of(rows)
    return lane >= LANE - ZB, lane < ZB, lane % ZB == ZB - 1, lane % ZB == 0


def own_part_kernel(potential, own, out, field, diag):
    planes, rows, columns = own.shape

    @pl.when(pl.program_id(0) == 0)
    def _():
        for p in (0, 1, planes + 2, planes + 3):
            field[p] = jnp.zeros((rows, columns), jnp.float32)
        for p in range(planes):
            diag[p] = jnp.broadcast_to(scaled_potential(potential[p : p + 1, :]), (rows, columns))

    field[2 : planes + 2] = own[...]
    masks = shift_masks(rows)

    def one_plane(p, _):
        def emit(j, center, near, far):
            out[p, :, piece(j)] = diag[p, :, piece(j)] * center + NEAR * near + FAR * far

        stencil_row(field, p, masks, emit)
        return 0

    lax.fori_loop(0, planes, one_plane, 0)


def own_part(potential, own):
    planes, count, columns = own.shape
    spec = pl.BlockSpec((planes, ROWS, columns), lambda i: (0, i, 0))
    return pl.pallas_call(
        own_part_kernel,
        grid=(count // ROWS,),
        in_specs=[whole_spec(potential.shape), spec],
        out_specs=spec,
        out_shape=jax.ShapeDtypeStruct(own.shape, own.dtype),
        scratch_shapes=[
            pltpu.VMEM((planes + 4, ROWS, columns), jnp.float32),
            pltpu.VMEM((planes, ROWS, columns), jnp.float32),
        ],
        compiler_params=pltpu.CompilerParams(vmem_limit_bytes=VMEM_LIMIT),
        cost_estimate=pl.CostEstimate(flops=1, bytes_accessed=1, transcendentals=0),
    )(potential, own)


def two_steps_kernel(last, count_done, *refs):
    done = refs[:count_done]
    place, from_mate, own, from_other, potential, partial, *rest = refs[count_done:]
    if last:
        first, out, field, inner, diag, held_all = rest
    else:
        out, to_mate, to_other, field, inner, diag = rest
    planes, rows, columns = own.shape

    @pl.when(pl.program_id(0) == 0)
    def _():
        for p in range(planes + 4):
            diag[p] = jnp.broadcast_to(potential[p : p + 1, :], (rows, columns))

    unpack_halo(from_mate, place[2], field)
    field[planes : 2 * planes] = own[...]
    unpack_halo(from_other, 1 - place[2], field)

    masks = shift_masks(rows)
    group = lanes_of(rows) // ZB
    odd = group % 2 == 1
    upper = group >= 2

    def first_stage(q, _):
        p = q + jnp.where(q >= 2, planes, 0)
        here = jnp.where(q < 2, place[0], place[1]).astype(jnp.float32)
        near_by = here * NEAR
        far_by = here * FAR

        def emit(j, center, near, far):
            inner[p, :, piece(j)] = diag[p, :, piece(j)] * center + near_by * near + far_by * far

        stencil_row(field, p + planes - 4, masks, emit)
        return 0

    lax.fori_loop(0, 4, first_stage, 0)
    top = 2 * planes
    for at in range(0, columns, ROW_BLOCK):
        lanes = pl.ds(at, ROW_BLOCK)
        below = field[planes - 1, :, lanes]
        above = field[top, :, lanes]
        inner[2, :, lanes] = partial[0, :, lanes] + (NEAR * below + FAR * field[planes - 2, :, lanes])
        inner[3, :, lanes] = partial[1, :, lanes] + FAR * below
        inner[planes, :, lanes] = partial[planes - 2, :, lanes] + FAR * above
        inner[planes + 1, :, lanes] = partial[planes - 1, :, lanes] + (NEAR * above + FAR * field[top + 1, :, lanes])

    own_rows = pl.ds(pl.multiple_of(pl.program_id(0) * rows, rows), rows)

    def second_stage(p, _):
        held = []

        def emit(j, center, near, far):
            total = diag[p + 2, :, piece(j)] * center + NEAR * near + FAR * far
            total = 2.0 * total - field[p + planes, :, piece(j)]
            if not last:
                out[p, :, piece(j)] = total
                return
            held.append(2.0 * total - first[p, :, piece(j)])
            if len(held) == GROUPS:
                done = split_groups(held, odd, upper)
                for a in range(GROUPS):
                    held_all[GROUPS * p + a, own_rows, piece(j // GROUPS)] = done[a]
                held.clear()

        stencil_row(inner, p, masks, emit)
        return 0

    lax.fori_loop(0, planes, second_stage, 0)
    if not last:
        pack_halo(out, place[2], to_mate, to_other)
        return

    @pl.when(pl.program_id(0) == pl.num_programs(0) - 1)
    def _():
        def one_part(i, _):
            both = [x[i].astype(jnp.float32) for x in done] + [held_all[i]]
            out[i] = jnp.concatenate(both, axis=0).astype(jnp.bfloat16)
            return 0

        lax.fori_loop(0, out.shape[0], one_part, 0)


def two_steps(place, halo, own, potential, partial, first=None, done=()):
    planes, count, columns = own.shape
    last = first is not None
    spec = pl.BlockSpec((planes, ROWS, columns), lambda i: (0, i, 0))
    near = halo_shape(count, columns)
    out_shape = [jax.ShapeDtypeStruct(own.shape, own.dtype), near, near]
    out_spec = [spec, whole_spec(near.shape), whole_spec(near.shape)]
    scratch = [
        pltpu.VMEM((planes * 3, ROWS, columns), jnp.float32),
        pltpu.VMEM((planes + 4, ROWS, columns), jnp.float32),
        pltpu.VMEM((planes + 4, ROWS, columns), jnp.float32),
    ]
    if last:
        shape = (planes * GROUPS, count, columns // GROUPS)
        scratch.append(pltpu.VMEM(shape, jnp.float32))
        shape = (planes * GROUPS, count + sum(x.shape[1] for x in done), columns // GROUPS)
        out_shape = jax.ShapeDtypeStruct(shape, jnp.bfloat16)
        out_spec = pl.BlockSpec(shape, lambda i: (0, 0, 0))
    return pl.pallas_call(
        functools.partial(two_steps_kernel, last, len(done)),
        grid=(count // ROWS,),
        in_specs=[whole_spec(x.shape) for x in done]
        + [pl.BlockSpec(memory_space=pltpu.SMEM)]
        + [whole_spec(halo[0].shape), spec, whole_spec(halo[1].shape), whole_spec(potential.shape), spec]
        + [spec] * last,
        out_specs=out_spec,
        out_shape=out_shape,
        scratch_shapes=scratch,
        compiler_params=pltpu.CompilerParams(vmem_limit_bytes=VMEM_LIMIT),
        cost_estimate=pl.CostEstimate(flops=1, bytes_accessed=1, transcendentals=0),
    )(*done, place, halo[0], own, halo[1], potential, partial, *([first] if last else []))


def z_order():
    one = np.zeros((NZ, NZ), np.float32)
    for z in range(NZ):
        one[z % ZI * ZB + z // ZI, z] = 1.0
    return jnp.asarray(np.kron(np.eye(GROUPS, dtype=np.float32), one), jnp.bfloat16)


def rotate_kernel(weights, cells, order, out):
    for k in range(cells.shape[1] // ROW_BLOCK):
        at = pl.ds(k * ROW_BLOCK, ROW_BLOCK)
        summed = jnp.dot(weights[...], cells[:, at], preferred_element_type=jnp.float32).astype(jnp.bfloat16)
        out[:, at] = jnp.dot(summed, order[...], preferred_element_type=jnp.float32).astype(jnp.bfloat16)


def rotate(weights, cells):
    return pl.pallas_call(
        rotate_kernel,
        out_shape=jax.ShapeDtypeStruct((weights.shape[0], cells.shape[1]), jnp.bfloat16),
        compiler_params=pltpu.CompilerParams(vmem_limit_bytes=VMEM_LIMIT),
        cost_estimate=pl.CostEstimate(flops=1, bytes_accessed=1, transcendentals=0),
    )(weights, cells, z_order())


def from_parts_kernel(parts, out, mixed):
    rows, planes, columns = out.shape
    width = parts.shape[2]
    groups = columns // width
    for p in range(planes):
        for a in range(groups):
            x = parts[p * groups + a].astype(jnp.float32)
            for j in range(width // LANE):
                for o in range(0, rows, ROWS):
                    at = pl.ds(o * planes + p, ROWS, stride=planes)
                    mixed[a * (width // LANE) + j, at, :] = x[o : o + ROWS, j * LANE : (j + 1) * LANE]
    for j in range(columns // LANE):
        out[:, :, piece(j)] = mixed[j].reshape(rows, planes, LANE)


def from_parts(parts, planes):
    n, count, width = parts.shape
    columns = n // planes * width
    return pl.pallas_call(
        from_parts_kernel,
        grid=(1,),
        in_specs=[pl.BlockSpec(parts.shape, lambda i: (0, 0, 0))],
        out_specs=pl.BlockSpec((count, planes, columns), lambda i: (0, 0, 0)),
        out_shape=jax.ShapeDtypeStruct((count, planes, columns), jnp.float32),
        scratch_shapes=[pltpu.VMEM((columns // LANE, count * planes, LANE), jnp.float32)],
        compiler_params=pltpu.CompilerParams(vmem_limit_bytes=VMEM_LIMIT),
        cost_estimate=pl.CostEstimate(flops=1, bytes_accessed=1, transcendentals=0),
    )(parts)


def body(orbitals, potential, rotation):
    count, planes, columns = orbitals.shape
    domains = lax.axis_size("space")
    members = lax.axis_size("band")
    mates = [(i, i ^ 1) for i in range(domains)]
    others = [(i, i + 1) for i in range(1, domains - 1, 2)]
    others = others + [(j, i) for i, j in others]

    def around(to_mate, to_other):
        other = lax.ppermute(to_other, "space", others)
        return lax.ppermute(to_mate, "space", mates), other

    at = lax.axis_index("space")
    place = jnp.stack([at > 0, at < domains - 1, at % 2]).astype(jnp.int32)

    orbitals = pltpu.with_memory_space_constraint(orbitals, pltpu.HBM)
    potential = pltpu.with_memory_space_constraint(potential, pltpu.HBM)
    starts = [sum(CHUNKS[:i]) for i in range(len(CHUNKS))]
    zeroth, halos = [], []
    for i, (start, chunk) in enumerate(zip(starts, CHUNKS)):
        fields, *halo = to_runs(place, orbitals, start, chunk, potential if i == 0 else None)
        if i == 0:
            field = halo.pop()
        zeroth.append(fields)
        halos.append(around(*halo))

    runs = field
    partials = [own_part(runs, x) for x in zeroth]
    fields_0, waited = lax.optimization_barrier((zeroth[0], halos[1][0]))
    halos[1] = (waited, halos[1][1])
    field = potential_field(place, halos[0], runs)
    second, next_halos = [], []
    for halo, fields, partial in zip(halos, (fields_0, zeroth[1]), partials):
        fields, *halo = two_steps(place, halo, fields, field, partial)
        second.append(fields)
        next_halos.append(around(*halo))
    partials = [own_part(runs, x) for x in second]
    filtered = ()
    for fields, halo, partial, first in zip(second, next_halos, partials, zeroth):
        filtered = (two_steps(place, halo, fields, field, partial, first, filtered),)
    filtered, = filtered
    gathered = lax.all_to_all(filtered, "band", 0, 0)
    width = columns // GROUPS
    summed = rotate(rotation.T, gathered.reshape(members * count, width))
    back = lax.all_to_all(summed.reshape(members, count, width), "band", 0, 0)
    return from_parts(back, planes)


def solution(mesh):
    return jax.shard_map(
        body,
        mesh=mesh,
        in_specs=(P("band", "space", None), P("space", None), P()),
        out_specs=P("band", "space", None),
        check_vma=False,
    )
```

```python
import functools

import jax
import jax.numpy as jnp
import numpy as np
from jax import lax
from jax.experimental import pallas as pl
from jax.experimental.pallas import tpu as pltpu
from jax.sharding import PartitionSpec as P

NY = 48
NZ = 96
LANE = 128
ROWS = 8
GROUPS = 4
RUNS = NY // GROUPS
ZI = 3
ZB = NZ // ZI
PIECES = RUNS * ZI
TERMS = 5
ROW_BLOCK = GROUPS * NZ
VMEM_LIMIT = 18 * 1024 * 1024
CHUNKS = (16, 8)

CENTER = 4.75
HALF_WIDTH = 3.75
NEAR = -2.0 / 3.0 / HALF_WIDTH
FAR = 1.0 / 24.0 / HALF_WIDTH


def lanes_of(rows):
    return lax.broadcasted_iota(jnp.int32, (rows, LANE), 1)


def piece(j):
    return pl.ds(j * LANE, LANE)


def split_groups(four, odd, upper):
    half = {}
    for i in (0, 2):
        half[i] = jnp.where(odd, pltpu.roll(four[i + 1], ZB, 1), four[i])
        half[i + 1] = jnp.where(odd, four[i + 1], pltpu.roll(four[i], LANE - ZB, 1))
    done = {}
    for i in (0, 1):
        done[i] = jnp.where(upper, pltpu.roll(half[i + 2], 2 * ZB, 1), half[i])
        done[i + 2] = jnp.where(upper, half[i + 2], pltpu.roll(half[i], 2 * ZB, 1))
    return done


def rounded(x):
    return x.astype(jnp.bfloat16).astype(jnp.float32)


def pack_halo(planes, odd, to_mate, to_other):
    half = PIECES // 2
    base = pl.program_id(0) * (TERMS * half * LANE)

    def put(to, term, j, low, high):
        at = pl.ds(pl.multiple_of(base + (term * half + j) * LANE, LANE), LANE)
        to[:, at] = jnp.concatenate([low, high], axis=0).astype(jnp.bfloat16)

    for to, upward in ((to_mate, 1 - odd), (to_other, odd)):
        order = [jnp.where(upward == 1, 3 - k, k) for k in range(4)]
        for j in range(half):
            for k, p in enumerate(order):
                low, high = planes[p, :, piece(j)], planes[p, :, piece(j + half)]
                put(to, k + min(k, 1), j, low, high)
                if k == 0:
                    put(to, 1, j, low - rounded(low), high - rounded(high))


def unpack_halo(halo, below, field):
    half = PIECES // 2
    base = pl.program_id(0) * (TERMS * half * LANE)
    order = [jnp.where(below == 1, 3 - k, 8 + k) for k in range(4)]

    def get(term, j):
        at = pl.ds(pl.multiple_of(base + (term * half + j) * LANE, LANE), LANE)
        return halo[:, at].astype(jnp.float32)

    for j in range(half):
        for k, p in enumerate(order):
            both = get(0, j) + get(1, j) if k == 0 else get(k + 1, j)
            field[p, :, piece(j)] = both[:ROWS]
            field[p, :, piece(j + half)] = both[ROWS:]


def halo_shape(count, columns, extra=0):
    lanes = count // ROWS * TERMS * columns // 2 + extra * columns // GROUPS
    return jax.ShapeDtypeStruct((2 * ROWS, lanes), jnp.bfloat16)


def whole_spec(shape):
    return pl.BlockSpec(shape, lambda i: (0,) * len(shape))


def split_terms(x, terms, at):
    first = rounded(x)
    second = rounded(x - first)
    terms[0, at] = first.astype(jnp.bfloat16)
    terms[1, at] = second.astype(jnp.bfloat16)
    terms[2, at] = (x - first - second).astype(jnp.bfloat16)


def reordered(terms, order):
    parts = [jnp.dot(terms[i], order[...], preferred_element_type=jnp.float32) for i in range(3)]
    return parts[0] + (parts[1] + parts[2])


def potential_to_runs(cells, odd, order, out, to_mate, to_other, gathered, terms, quarters):
    planes, columns = cells.shape
    blocks = columns // ROW_BLOCK
    for k in range(blocks):
        x = cells[:, pl.ds(k * ROW_BLOCK, ROW_BLOCK)]
        gathered[pl.ds(k * ROWS, ROWS), :] = jnp.concatenate([x, jnp.zeros_like(x)], axis=0)
    split_terms(gathered[...], terms, pl.ds(0, blocks * ROWS))
    gathered[...] = reordered(terms, order)
    group = lanes_of(ROWS) // ZB
    per_group = blocks // GROUPS
    for m in range(PIECES // GROUPS):
        four = [gathered[pl.ds((a * per_group + m // ZI) * ROWS, ROWS), piece(m % ZI)] for a in range(GROUPS)]
        done = split_groups(four, group % 2 == 1, group >= 2)
        for i in range(GROUPS):
            x = done[i]
            j = GROUPS * m + i
            out[:, piece(j)] = x[:planes]
            quarter, lanes = j // (PIECES // GROUPS), piece(j % (PIECES // GROUPS))
            for to, upward in ((0, 1 - odd), (1, odd)):
                near = jnp.where(upward == 1, x[planes - 1 : planes], x[0:1])
                next_near = jnp.where(upward == 1, x[planes - 2 : planes - 1], x[1:2])
                rows = [near, near - rounded(near), next_near, next_near - rounded(next_near)]
                for r, row in enumerate(rows):
                    quarters[to, GROUPS * r + quarter : GROUPS * r + quarter + 1, lanes] = row
    width = columns // GROUPS
    for i, to in enumerate((to_mate, to_other)):
        to[:, to.shape[1] - width : to.shape[1]] = quarters[i].astype(jnp.bfloat16)


def to_runs_kernel(extra, place, cells, *rest):
    if extra:
        potential, out, to_mate, to_other, runs, order, terms, turned, gathered, few_terms, quarters = rest
    else:
        out, to_mate, to_other, order, terms, turned = rest
    planes, rows, columns = out.shape
    blocks = columns // ROW_BLOCK

    @pl.when(pl.program_id(0) == 0)
    def _():
        to = lax.broadcasted_iota(jnp.int32, order.shape, 1)
        source = to // NZ * NZ + to % ZB * ZI + to % NZ // ZB
        order[...] = jnp.where(lax.broadcasted_iota(jnp.int32, order.shape, 0) == source, 1.0, 0.0).astype(jnp.bfloat16)
        if extra:
            potential_to_runs(potential, place[2], order, runs, to_mate, to_other, gathered, few_terms, quarters)

    for k in range(blocks):
        x = cells[:, :, pl.ds(k * ROW_BLOCK, ROW_BLOCK)].reshape(rows * planes, ROW_BLOCK)
        split_terms(x, terms, pl.ds(k * rows * planes, rows * planes))
    whole = reordered(terms, order)
    for zi in range(ZI):
        turned[zi] = whole[:, zi * LANE : (zi + 1) * LANE]

    group = lanes_of(rows) // ZB
    odd = group % 2 == 1
    upper = group >= 2
    per_group = blocks // GROUPS
    for m in range(PIECES // GROUPS):
        for p in range(planes):
            four = []
            for a in range(GROUPS):
                k = a * per_group + m // ZI
                four.append(turned[m % ZI, pl.ds(k * rows * planes + p, rows, stride=planes), :])
            done = split_groups(four, odd, upper)
            for i in range(GROUPS):
                out[p, :, piece(GROUPS * m + i)] = done[i]
    pack_halo(out, place[2], to_mate, to_other)


def to_runs(place, cells, start, count, potential=None):
    _, planes, columns = cells.shape
    extra = potential is not None
    halo = halo_shape(count, columns, int(extra))
    blocks = columns // ROW_BLOCK
    total = planes * ROWS * blocks
    scratch = [
        pltpu.VMEM((ROW_BLOCK, ROW_BLOCK), jnp.bfloat16),
        pltpu.VMEM((3, total, ROW_BLOCK), jnp.bfloat16),
        pltpu.VMEM((ZI, total, LANE), jnp.float32),
    ]
    if extra:
        scratch.append(pltpu.VMEM((blocks * ROWS, ROW_BLOCK), jnp.float32))
        scratch.append(pltpu.VMEM((3, blocks * ROWS, ROW_BLOCK), jnp.bfloat16))
        scratch.append(pltpu.VMEM((2, 4 * GROUPS, columns // GROUPS), jnp.float32))
    return pl.pallas_call(
        functools.partial(to_runs_kernel, extra),
        grid=(count // ROWS,),
        in_specs=[
            pl.BlockSpec(memory_space=pltpu.SMEM),
            pl.BlockSpec((ROWS, planes, columns), lambda i: (start // ROWS + i, 0, 0)),
        ]
        + [whole_spec((planes, columns))] * extra,
        out_specs=[pl.BlockSpec((planes, ROWS, columns), lambda i: (0, i, 0))]
        + [whole_spec(halo.shape)] * 2
        + [whole_spec((planes, columns))] * extra,
        out_shape=[pltpu.HBM((planes, count, columns), cells.dtype), halo, halo]
        + [jax.ShapeDtypeStruct((planes, columns), jnp.float32)] * extra,
        scratch_shapes=scratch,
        compiler_params=pltpu.CompilerParams(vmem_limit_bytes=VMEM_LIMIT),
        cost_estimate=pl.CostEstimate(flops=1, bytes_accessed=1, transcendentals=0),
    )(place, cells, *([potential] if extra else []))


def stencil_row(src, plane, masks, emit):
    a_last, a_first, zb_last, zb_first = masks
    centers, turned = {}, {}

    def center(b, zi):
        if (b, zi) not in centers:
            centers[b, zi] = src[plane + 2, :, piece(ZI * b + zi)]
        return centers[b, zi]

    def turn(b, zi, by, mask):
        if (b, zi, by) not in turned:
            turned[b, zi, by] = jnp.where(mask, 0.0, pltpu.roll(center(b, zi), by, 1))
        return turned[b, zi, by]

    def at_y(b, zi):
        if b < 0:
            return turn(b + RUNS, zi, ZB, a_first)
        if b >= RUNS:
            return turn(b - RUNS, zi, LANE - ZB, a_last)
        return center(b, zi)

    def at_z(b, zi):
        if zi < 0:
            return turn(b, zi + ZI, 1, zb_first)
        if zi >= ZI:
            return turn(b, zi - ZI, LANE - 1, zb_last)
        return center(b, zi)

    def at_x(j, k):
        return src[plane + 2 + k, :, piece(j)]

    for b in range(RUNS):
        for zi in range(ZI):
            j = ZI * b + zi
            near, far = [
                (at_x(j, -k) + at_x(j, k)) + (at_y(b - k, zi) + at_y(b + k, zi)) + (at_z(b, zi - k) + at_z(b, zi + k))
                for k in (1, 2)
            ]
            emit(j, center(b, zi), near, far)


def potential_field_kernel(place, from_mate, own, from_other, out):
    planes = own.shape[0]
    scale = scaled_potential
    out[2 : planes + 2] = scale(own[...])
    mate, other = [halo[...].astype(jnp.float32) for halo in (from_mate, from_other)]
    mate_below = place[2] == 1
    below = jnp.where(mate_below, mate, other)
    above = jnp.where(mate_below, other, mate)
    width = below.shape[1]
    rows = ((1, below, 0), (0, below, 2), (planes + 2, above, 0), (planes + 3, above, 2))
    for p, terms, first in rows:
        whole = terms[first * GROUPS : (first + 1) * GROUPS] + terms[(first + 1) * GROUPS : (first + 2) * GROUPS]
        for q in range(GROUPS):
            out[p : p + 1, q * width : (q + 1) * width] = scale(whole[q : q + 1])


def potential_field(place, halo, own):
    planes, columns = own.shape
    width = columns // GROUPS
    specs = [pl.BlockSpec((x.shape[0], width), lambda i, n=x.shape[1] // width: (0, n - 1)) for x in halo]
    return pl.pallas_call(
        potential_field_kernel,
        grid=(1,),
        in_specs=[pl.BlockSpec(memory_space=pltpu.SMEM), specs[0], whole_spec(own.shape), specs[1]],
        out_specs=whole_spec((planes + 4, columns)),
        out_shape=jax.ShapeDtypeStruct((planes + 4, columns), jnp.float32),
        compiler_params=pltpu.CompilerParams(vmem_limit_bytes=VMEM_LIMIT),
    )(place, halo[0], own, halo[1])


def scaled_potential(x):
    return (x + (HALF_WIDTH - CENTER)) / HALF_WIDTH


def shift_masks(rows):
    lane = lanes_of(rows)
    return lane >= LANE - ZB, lane < ZB, lane % ZB == ZB - 1, lane % ZB == 0


def own_part_kernel(potential, own, out, field, diag):
    planes, rows, columns = own.shape

    @pl.when(pl.program_id(0) == 0)
    def _():
        for p in (0, 1, planes + 2, planes + 3):
            field[p] = jnp.zeros((rows, columns), jnp.float32)
        for p in range(planes):
            diag[p] = jnp.broadcast_to(scaled_potential(potential[p : p + 1, :]), (rows, columns))

    field[2 : planes + 2] = own[...]
    masks = shift_masks(rows)

    def one_plane(p, _):
        def emit(j, center, near, far):
            out[p, :, piece(j)] = diag[p, :, piece(j)] * center + NEAR * near + FAR * far

        stencil_row(field, p, masks, emit)
        return 0

    lax.fori_loop(0, planes, one_plane, 0)


def own_part(potential, own):
    planes, count, columns = own.shape
    spec = pl.BlockSpec((planes, ROWS, columns), lambda i: (0, i, 0))
    return pl.pallas_call(
        own_part_kernel,
        grid=(count // ROWS,),
        in_specs=[whole_spec(potential.shape), spec],
        out_specs=spec,
        out_shape=jax.ShapeDtypeStruct(own.shape, own.dtype),
        scratch_shapes=[
            pltpu.VMEM((planes + 4, ROWS, columns), jnp.float32),
            pltpu.VMEM((planes, ROWS, columns), jnp.float32),
        ],
        compiler_params=pltpu.CompilerParams(vmem_limit_bytes=VMEM_LIMIT),
        cost_estimate=pl.CostEstimate(flops=1, bytes_accessed=1, transcendentals=0),
    )(potential, own)


def two_steps_kernel(last, count_done, *refs):
    done = refs[:count_done]
    place, from_mate, own, from_other, potential, partial, *rest = refs[count_done:]
    if last:
        first, out, field, inner, diag, held_all = rest
    else:
        out, to_mate, to_other, field, inner, diag = rest
    planes, rows, columns = own.shape

    @pl.when(pl.program_id(0) == 0)
    def _():
        for p in range(planes + 4):
            diag[p] = jnp.broadcast_to(potential[p : p + 1, :], (rows, columns))

    unpack_halo(from_mate, place[2], field)
    field[planes : 2 * planes] = own[...]
    unpack_halo(from_other, 1 - place[2], field)

    masks = shift_masks(rows)
    group = lanes_of(rows) // ZB
    odd = group % 2 == 1
    upper = group >= 2

    def first_stage(q, _):
        p = q + jnp.where(q >= 2, planes, 0)
        here = jnp.where(q < 2, place[0], place[1]).astype(jnp.float32)
        near_by = here * NEAR
        far_by = here * FAR

        def emit(j, center, near, far):
            inner[p, :, piece(j)] = diag[p, :, piece(j)] * center + near_by * near + far_by * far

        stencil_row(field, p + planes - 4, masks, emit)
        return 0

    lax.fori_loop(0, 4, first_stage, 0)
    top = 2 * planes
    for at in range(0, columns, ROW_BLOCK):
        lanes = pl.ds(at, ROW_BLOCK)
        below = field[planes - 1, :, lanes]
        above = field[top, :, lanes]
        inner[2, :, lanes] = partial[0, :, lanes] + (NEAR * below + FAR * field[planes - 2, :, lanes])
        inner[3, :, lanes] = partial[1, :, lanes] + FAR * below
        inner[planes, :, lanes] = partial[planes - 2, :, lanes] + FAR * above
        inner[planes + 1, :, lanes] = partial[planes - 1, :, lanes] + (NEAR * above + FAR * field[top + 1, :, lanes])

    own_rows = pl.ds(pl.multiple_of(pl.program_id(0) * rows, rows), rows)

    def second_stage(p, _):
        held = []

        def emit(j, center, near, far):
            total = diag[p + 2, :, piece(j)] * center + NEAR * near + FAR * far
            total = 2.0 * total - field[p + planes, :, piece(j)]
            if not last:
                out[p, :, piece(j)] = total
                return
            held.append(2.0 * total - first[p, :, piece(j)])
            if len(held) == GROUPS:
                done = split_groups(held, odd, upper)
                for a in range(GROUPS):
                    held_all[GROUPS * p + a, own_rows, piece(j // GROUPS)] = done[a]
                held.clear()

        stencil_row(inner, p, masks, emit)
        return 0

    lax.fori_loop(0, planes, second_stage, 0)
    if not last:
        pack_halo(out, place[2], to_mate, to_other)
        return

    @pl.when(pl.program_id(0) == pl.num_programs(0) - 1)
    def _():
        def one_part(i, _):
            both = [x[i].astype(jnp.float32) for x in done] + [held_all[i]]
            out[i] = jnp.concatenate(both, axis=0).astype(jnp.bfloat16)
            return 0

        lax.fori_loop(0, out.shape[0], one_part, 0)


def two_steps(place, halo, own, potential, partial, first=None, done=()):
    planes, count, columns = own.shape
    last = first is not None
    spec = pl.BlockSpec((planes, ROWS, columns), lambda i: (0, i, 0))
    near = halo_shape(count, columns)
    out_shape = [jax.ShapeDtypeStruct(own.shape, own.dtype), near, near]
    out_spec = [spec, whole_spec(near.shape), whole_spec(near.shape)]
    scratch = [
        pltpu.VMEM((planes * 3, ROWS, columns), jnp.float32),
        pltpu.VMEM((planes + 4, ROWS, columns), jnp.float32),
        pltpu.VMEM((planes + 4, ROWS, columns), jnp.float32),
    ]
    if last:
        shape = (planes * GROUPS, count, columns // GROUPS)
        scratch.append(pltpu.VMEM(shape, jnp.float32))
        shape = (planes * GROUPS, count + sum(x.shape[1] for x in done), columns // GROUPS)
        out_shape = jax.ShapeDtypeStruct(shape, jnp.bfloat16)
        out_spec = pl.BlockSpec(shape, lambda i: (0, 0, 0))
    return pl.pallas_call(
        functools.partial(two_steps_kernel, last, len(done)),
        grid=(count // ROWS,),
        in_specs=[whole_spec(x.shape) for x in done]
        + [pl.BlockSpec(memory_space=pltpu.SMEM)]
        + [whole_spec(halo[0].shape), spec, whole_spec(halo[1].shape), whole_spec(potential.shape), spec]
        + [spec] * last,
        out_specs=out_spec,
        out_shape=out_shape,
        scratch_shapes=scratch,
        compiler_params=pltpu.CompilerParams(vmem_limit_bytes=VMEM_LIMIT),
        cost_estimate=pl.CostEstimate(flops=1, bytes_accessed=1, transcendentals=0),
    )(*done, place, halo[0], own, halo[1], potential, partial, *([first] if last else []))


def z_order():
    one = np.zeros((NZ, NZ), np.float32)
    for z in range(NZ):
        one[z % ZI * ZB + z // ZI, z] = 1.0
    return jnp.asarray(np.kron(np.eye(GROUPS, dtype=np.float32), one), jnp.bfloat16)


def rotate_kernel(weights, cells, order, out):
    for k in range(cells.shape[1] // ROW_BLOCK):
        at = pl.ds(k * ROW_BLOCK, ROW_BLOCK)
        summed = jnp.dot(weights[...], cells[:, at], preferred_element_type=jnp.float32).astype(jnp.bfloat16)
        out[:, at] = jnp.dot(summed, order[...], preferred_element_type=jnp.float32).astype(jnp.bfloat16)


def rotate(weights, cells):
    return pl.pallas_call(
        rotate_kernel,
        out_shape=jax.ShapeDtypeStruct((weights.shape[0], cells.shape[1]), jnp.bfloat16),
        compiler_params=pltpu.CompilerParams(vmem_limit_bytes=VMEM_LIMIT),
        cost_estimate=pl.CostEstimate(flops=1, bytes_accessed=1, transcendentals=0),
    )(weights, cells, z_order())


def from_parts_kernel(parts, out, mixed):
    rows, planes, columns = out.shape
    width = parts.shape[2]
    groups = columns // width
    for p in range(planes):
        for a in range(groups):
            x = parts[p * groups + a].astype(jnp.float32)
            for j in range(width // LANE):
                for o in range(0, rows, ROWS):
                    at = pl.ds(o * planes + p, ROWS, stride=planes)
                    mixed[a * (width // LANE) + j, at, :] = x[o : o + ROWS, j * LANE : (j + 1) * LANE]
    for j in range(columns // LANE):
        out[:, :, piece(j)] = mixed[j].reshape(rows, planes, LANE)


def from_parts(parts, planes):
    n, count, width = parts.shape
    columns = n // planes * width
    return pl.pallas_call(
        from_parts_kernel,
        grid=(1,),
        in_specs=[pl.BlockSpec(parts.shape, lambda i: (0, 0, 0))],
        out_specs=pl.BlockSpec((count, planes, columns), lambda i: (0, 0, 0)),
        out_shape=jax.ShapeDtypeStruct((count, planes, columns), jnp.float32),
        scratch_shapes=[pltpu.VMEM((columns // LANE, count * planes, LANE), jnp.float32)],
        compiler_params=pltpu.CompilerParams(vmem_limit_bytes=VMEM_LIMIT),
        cost_estimate=pl.CostEstimate(flops=1, bytes_accessed=1, transcendentals=0),
    )(parts)


def body(orbitals, potential, rotation):
    count, planes, columns = orbitals.shape
    domains = lax.axis_size("space")
    members = lax.axis_size("band")
    mates = [(i, i ^ 1) for i in range(domains)]
    others = [(i, i + 1) for i in range(1, domains - 1, 2)]
    others = others + [(j, i) for i, j in others]

    def around(to_mate, to_other):
        other = lax.ppermute(to_other, "space", others)
        return lax.ppermute(to_mate, "space", mates), other

    at = lax.axis_index("space")
    place = jnp.stack([at > 0, at < domains - 1, at % 2]).astype(jnp.int32)

    orbitals = pltpu.with_memory_space_constraint(orbitals, pltpu.HBM)
    potential = pltpu.with_memory_space_constraint(potential, pltpu.HBM)
    starts = [sum(CHUNKS[:i]) for i in range(len(CHUNKS))]
    zeroth, halos = [], []
    for i, (start, chunk) in enumerate(zip(starts, CHUNKS)):
        fields, *halo = to_runs(place, orbitals, start, chunk, potential if i == 0 else None)
        if i == 0:
            field = halo.pop()
        zeroth.append(fields)
        halos.append(around(*halo))

    runs = field
    partials = [own_part(runs, x) for x in zeroth]
    fields_0, waited = lax.optimization_barrier((zeroth[0], halos[1][0]))
    halos[1] = (waited, halos[1][1])
    field = potential_field(place, halos[0], runs)
    second, next_halos = [], []
    for halo, fields, partial in zip(halos, (fields_0, zeroth[1]), partials):
        fields, *halo = two_steps(place, halo, fields, field, partial)
        second.append(fields)
        next_halos.append(around(*halo))
    partials = [own_part(runs, x) for x in second]
    filtered = ()
    for fields, halo, partial, first in zip(second, next_halos, partials, zeroth):
        filtered = (two_steps(place, halo, fields, field, partial, first, filtered),)
    filtered, = filtered
    gathered = lax.all_to_all(filtered, "band", 0, 0)
    width = columns // GROUPS
    summed = rotate(rotation.T, gathered.reshape(members * count, width))
    back = lax.all_to_all(summed.reshape(members, count, width), "band", 0, 0)
    return from_parts(back, planes)


def solution(mesh):
    return jax.shard_map(
        body,
        mesh=mesh,
        in_specs=(P("band", "space", None), P("space", None), P()),
        out_specs=P("band", "space", None),
        check_vma=False,
    )
```

```python
import functools

import jax
import jax.numpy as jnp
import numpy as np
from jax import lax
from jax.experimental import pallas as pl
from jax.experimental.pallas import tpu as pltpu
from jax.sharding import PartitionSpec as P

NY = 48
NZ = 96
LANE = 128
ROWS = 8
GROUPS = 4
RUNS = NY // GROUPS
ZI = 3
ZB = NZ // ZI
PIECES = RUNS * ZI
TERMS = 5
ROW_BLOCK = GROUPS * NZ
VMEM_LIMIT = 14 * 1024 * 1024
CHUNKS = (16, 8)

CENTER = 4.75
HALF_WIDTH = 3.75
NEAR = -2.0 / 3.0 / HALF_WIDTH
FAR = 1.0 / 24.0 / HALF_WIDTH


def lanes_of(rows):
    return lax.broadcasted_iota(jnp.int32, (rows, LANE), 1)


def piece(j):
    return pl.ds(j * LANE, LANE)


def split_groups(four, odd, upper):
    half = {}
    for i in (0, 2):
        half[i] = jnp.where(odd, pltpu.roll(four[i + 1], ZB, 1), four[i])
        half[i + 1] = jnp.where(odd, four[i + 1], pltpu.roll(four[i], LANE - ZB, 1))
    done = {}
    for i in (0, 1):
        done[i] = jnp.where(upper, pltpu.roll(half[i + 2], 2 * ZB, 1), half[i])
        done[i + 2] = jnp.where(upper, half[i + 2], pltpu.roll(half[i], 2 * ZB, 1))
    return done


def rounded(x):
    return x.astype(jnp.bfloat16).astype(jnp.float32)


def pack_halo(planes, odd, to_mate, to_other):
    half = PIECES // 2
    base = pl.program_id(0) * (TERMS * half * LANE)

    def put(to, term, j, low, high):
        at = pl.ds(pl.multiple_of(base + (term * half + j) * LANE, LANE), LANE)
        to[:, at] = jnp.concatenate([low, high], axis=0).astype(jnp.bfloat16)

    for to, upward in ((to_mate, 1 - odd), (to_other, odd)):
        order = [jnp.where(upward == 1, 3 - k, k) for k in range(4)]
        for j in range(half):
            for k, p in enumerate(order):
                low, high = planes[p, :, piece(j)], planes[p, :, piece(j + half)]
                put(to, k + min(k, 1), j, low, high)
                if k == 0:
                    put(to, 1, j, low - rounded(low), high - rounded(high))


def unpack_halo(halo, below, field):
    half = PIECES // 2
    base = pl.program_id(0) * (TERMS * half * LANE)
    order = [jnp.where(below == 1, 3 - k, 8 + k) for k in range(4)]

    def get(term, j):
        at = pl.ds(pl.multiple_of(base + (term * half + j) * LANE, LANE), LANE)
        return halo[:, at].astype(jnp.float32)

    for j in range(half):
        for k, p in enumerate(order):
            both = get(0, j) + get(1, j) if k == 0 else get(k + 1, j)
            field[p, :, piece(j)] = both[:ROWS]
            field[p, :, piece(j + half)] = both[ROWS:]


def halo_shape(count, columns, extra=0):
    lanes = count // ROWS * TERMS * columns // 2 + extra * columns // GROUPS
    return jax.ShapeDtypeStruct((2 * ROWS, lanes), jnp.bfloat16)


def whole_spec(shape):
    return pl.BlockSpec(shape, lambda i: (0,) * len(shape))


def split_terms(x, terms, at):
    first = rounded(x)
    second = rounded(x - first)
    terms[0, at] = first.astype(jnp.bfloat16)
    terms[1, at] = second.astype(jnp.bfloat16)
    terms[2, at] = (x - first - second).astype(jnp.bfloat16)


def reordered(terms, order):
    parts = [jnp.dot(terms[i], order[...], preferred_element_type=jnp.float32) for i in range(3)]
    return parts[0] + (parts[1] + parts[2])


def potential_to_runs(cells, odd, order, out, to_mate, to_other, gathered, terms, quarters):
    planes, columns = cells.shape
    blocks = columns // ROW_BLOCK
    for k in range(blocks):
        x = cells[:, pl.ds(k * ROW_BLOCK, ROW_BLOCK)]
        gathered[pl.ds(k * ROWS, ROWS), :] = jnp.concatenate([x, jnp.zeros_like(x)], axis=0)
    split_terms(gathered[...], terms, pl.ds(0, blocks * ROWS))
    gathered[...] = reordered(terms, order)
    group = lanes_of(ROWS) // ZB
    per_group = blocks // GROUPS
    for m in range(PIECES // GROUPS):
        four = [gathered[pl.ds((a * per_group + m // ZI) * ROWS, ROWS), piece(m % ZI)] for a in range(GROUPS)]
        done = split_groups(four, group % 2 == 1, group >= 2)
        for i in range(GROUPS):
            x = done[i]
            j = GROUPS * m + i
            out[:, piece(j)] = x[:planes]
            quarter, lanes = j // (PIECES // GROUPS), piece(j % (PIECES // GROUPS))
            for to, upward in ((0, 1 - odd), (1, odd)):
                near = jnp.where(upward == 1, x[planes - 1 : planes], x[0:1])
                next_near = jnp.where(upward == 1, x[planes - 2 : planes - 1], x[1:2])
                rows = [near, near - rounded(near), next_near, next_near - rounded(next_near)]
                for r, row in enumerate(rows):
                    quarters[to, GROUPS * r + quarter : GROUPS * r + quarter + 1, lanes] = row
    width = columns // GROUPS
    for i, to in enumerate((to_mate, to_other)):
        to[:, to.shape[1] - width : to.shape[1]] = quarters[i].astype(jnp.bfloat16)


def to_runs_kernel(extra, place, cells, *rest):
    if extra:
        potential, out, to_mate, to_other, runs, order, terms, turned, gathered, few_terms, quarters = rest
    else:
        out, to_mate, to_other, order, terms, turned = rest
    planes, rows, columns = out.shape
    blocks = columns // ROW_BLOCK

    @pl.when(pl.program_id(0) == 0)
    def _():
        to = lax.broadcasted_iota(jnp.int32, order.shape, 1)
        source = to // NZ * NZ + to % ZB * ZI + to % NZ // ZB
        order[...] = jnp.where(lax.broadcasted_iota(jnp.int32, order.shape, 0) == source, 1.0, 0.0).astype(jnp.bfloat16)
        if extra:
            potential_to_runs(potential, place[2], order, runs, to_mate, to_other, gathered, few_terms, quarters)

    for k in range(blocks):
        x = cells[:, :, pl.ds(k * ROW_BLOCK, ROW_BLOCK)].reshape(rows * planes, ROW_BLOCK)
        split_terms(x, terms, pl.ds(k * rows * planes, rows * planes))
    whole = reordered(terms, order)
    for zi in range(ZI):
        turned[zi] = whole[:, zi * LANE : (zi + 1) * LANE]

    group = lanes_of(rows) // ZB
    odd = group % 2 == 1
    upper = group >= 2
    per_group = blocks // GROUPS
    for m in range(PIECES // GROUPS):
        for p in range(planes):
            four = []
            for a in range(GROUPS):
                k = a * per_group + m // ZI
                four.append(turned[m % ZI, pl.ds(k * rows * planes + p, rows, stride=planes), :])
            done = split_groups(four, odd, upper)
            for i in range(GROUPS):
                out[p, :, piece(GROUPS * m + i)] = done[i]
    pack_halo(out, place[2], to_mate, to_other)


def to_runs(place, cells, start, count, potential=None):
    _, planes, columns = cells.shape
    extra = potential is not None
    halo = halo_shape(count, columns, int(extra))
    blocks = columns // ROW_BLOCK
    total = planes * ROWS * blocks
    scratch = [
        pltpu.VMEM((ROW_BLOCK, ROW_BLOCK), jnp.bfloat16),
        pltpu.VMEM((3, total, ROW_BLOCK), jnp.bfloat16),
        pltpu.VMEM((ZI, total, LANE), jnp.float32),
    ]
    if extra:
        scratch.append(pltpu.VMEM((blocks * ROWS, ROW_BLOCK), jnp.float32))
        scratch.append(pltpu.VMEM((3, blocks * ROWS, ROW_BLOCK), jnp.bfloat16))
        scratch.append(pltpu.VMEM((2, 4 * GROUPS, columns // GROUPS), jnp.float32))
    return pl.pallas_call(
        functools.partial(to_runs_kernel, extra),
        grid=(count // ROWS,),
        in_specs=[
            pl.BlockSpec(memory_space=pltpu.SMEM),
            pl.BlockSpec((ROWS, planes, columns), lambda i: (start // ROWS + i, 0, 0)),
        ]
        + [whole_spec((planes, columns))] * extra,
        out_specs=[pl.BlockSpec((planes, ROWS, columns), lambda i: (0, i, 0))]
        + [whole_spec(halo.shape)] * 2
        + [whole_spec((planes, columns))] * extra,
        out_shape=[pltpu.HBM((planes, count, columns), cells.dtype), halo, halo]
        + [jax.ShapeDtypeStruct((planes, columns), jnp.float32)] * extra,
        scratch_shapes=scratch,
        compiler_params=pltpu.CompilerParams(vmem_limit_bytes=VMEM_LIMIT),
        cost_estimate=pl.CostEstimate(flops=1, bytes_accessed=1, transcendentals=0),
    )(place, cells, *([potential] if extra else []))


def stencil_row(src, plane, masks, emit):
    a_last, a_first, zb_last, zb_first = masks
    centers, turned = {}, {}

    def center(b, zi):
        if (b, zi) not in centers:
            centers[b, zi] = src[plane + 2, :, piece(ZI * b + zi)]
        return centers[b, zi]

    def turn(b, zi, by, mask):
        if (b, zi, by) not in turned:
            turned[b, zi, by] = jnp.where(mask, 0.0, pltpu.roll(center(b, zi), by, 1))
        return turned[b, zi, by]

    def at_y(b, zi):
        if b < 0:
            return turn(b + RUNS, zi, ZB, a_first)
        if b >= RUNS:
            return turn(b - RUNS, zi, LANE - ZB, a_last)
        return center(b, zi)

    def at_z(b, zi):
        if zi < 0:
            return turn(b, zi + ZI, 1, zb_first)
        if zi >= ZI:
            return turn(b, zi - ZI, LANE - 1, zb_last)
        return center(b, zi)

    def at_x(j, k):
        return src[plane + 2 + k, :, piece(j)]

    for b in range(RUNS):
        for zi in range(ZI):
            j = ZI * b + zi
            near, far = [
                (at_x(j, -k) + at_x(j, k)) + (at_y(b - k, zi) + at_y(b + k, zi)) + (at_z(b, zi - k) + at_z(b, zi + k))
                for k in (1, 2)
            ]
            emit(j, center(b, zi), near, far)


def potential_field_kernel(place, from_mate, own, from_other, out):
    planes = own.shape[0]
    scale = scaled_potential
    out[2 : planes + 2] = scale(own[...])
    mate, other = [halo[...].astype(jnp.float32) for halo in (from_mate, from_other)]
    mate_below = place[2] == 1
    below = jnp.where(mate_below, mate, other)
    above = jnp.where(mate_below, other, mate)
    width = below.shape[1]
    rows = ((1, below, 0), (0, below, 2), (planes + 2, above, 0), (planes + 3, above, 2))
    for p, terms, first in rows:
        whole = terms[first * GROUPS : (first + 1) * GROUPS] + terms[(first + 1) * GROUPS : (first + 2) * GROUPS]
        for q in range(GROUPS):
            out[p : p + 1, q * width : (q + 1) * width] = scale(whole[q : q + 1])


def scaled_potential(x):
    return (x + (HALF_WIDTH - CENTER)) / HALF_WIDTH


def shift_masks(rows):
    lane = lanes_of(rows)
    return lane >= LANE - ZB, lane < ZB, lane % ZB == ZB - 1, lane % ZB == 0


def own_part_kernel(potential, own, out, field, diag):
    planes, rows, columns = own.shape

    @pl.when(pl.program_id(0) == 0)
    def _():
        for p in (0, 1, planes + 2, planes + 3):
            field[p] = jnp.zeros((rows, columns), jnp.float32)
        for p in range(planes):
            diag[p] = jnp.broadcast_to(scaled_potential(potential[p : p + 1, :]), (rows, columns))

    field[2 : planes + 2] = own[...]
    masks = shift_masks(rows)

    def one_plane(p, _):
        def emit(j, center, near, far):
            out[p, :, piece(j)] = diag[p, :, piece(j)] * center + NEAR * near + FAR * far

        stencil_row(field, p, masks, emit)
        return 0

    lax.fori_loop(0, planes, one_plane, 0)


def own_part(potential, own):
    planes, count, columns = own.shape
    spec = pl.BlockSpec((planes, ROWS, columns), lambda i: (0, i, 0))
    return pl.pallas_call(
        own_part_kernel,
        grid=(count // ROWS,),
        in_specs=[whole_spec(potential.shape), spec],
        out_specs=spec,
        out_shape=jax.ShapeDtypeStruct(own.shape, own.dtype),
        scratch_shapes=[
            pltpu.VMEM((planes + 4, ROWS, columns), jnp.float32),
            pltpu.VMEM((planes, ROWS, columns), jnp.float32),
        ],
        compiler_params=pltpu.CompilerParams(vmem_limit_bytes=VMEM_LIMIT),
        cost_estimate=pl.CostEstimate(flops=1, bytes_accessed=1, transcendentals=0),
    )(potential, own)


def two_steps_kernel(last, extra, count_done, *refs):
    done = refs[:count_done]
    place, from_mate, own, from_other, potential, partial, *rest = refs[count_done:]
    if extra:
        runs, (mate_end, other_end, out, to_mate, to_other, potential, *rest) = potential, rest
        rest = (out, to_mate, to_other, *rest)
    if last:
        first, out, field, inner, diag, held_all = rest
    else:
        out, to_mate, to_other, field, inner, diag = rest
    planes, rows, columns = own.shape

    @pl.when(pl.program_id(0) == 0)
    def _():
        if extra:
            potential_field_kernel(place, mate_end, runs, other_end, potential)
        for p in range(planes + 4):
            diag[p] = jnp.broadcast_to(potential[p : p + 1, :], (rows, columns))

    unpack_halo(from_mate, place[2], field)
    field[planes : 2 * planes] = own[...]
    unpack_halo(from_other, 1 - place[2], field)

    masks = shift_masks(rows)
    group = lanes_of(rows) // ZB
    odd = group % 2 == 1
    upper = group >= 2

    def first_stage(q, _):
        p = q + jnp.where(q >= 2, planes, 0)
        here = jnp.where(q < 2, place[0], place[1]).astype(jnp.float32)
        near_by = here * NEAR
        far_by = here * FAR

        def emit(j, center, near, far):
            inner[p, :, piece(j)] = diag[p, :, piece(j)] * center + near_by * near + far_by * far

        stencil_row(field, p + planes - 4, masks, emit)
        return 0

    lax.fori_loop(0, 4, first_stage, 0)
    top = 2 * planes
    for at in range(0, columns, ROW_BLOCK):
        lanes = pl.ds(at, ROW_BLOCK)
        below = field[planes - 1, :, lanes]
        above = field[top, :, lanes]
        inner[2, :, lanes] = partial[0, :, lanes] + (NEAR * below + FAR * field[planes - 2, :, lanes])
        inner[3, :, lanes] = partial[1, :, lanes] + FAR * below
        inner[planes, :, lanes] = partial[planes - 2, :, lanes] + FAR * above
        inner[planes + 1, :, lanes] = partial[planes - 1, :, lanes] + (NEAR * above + FAR * field[top + 1, :, lanes])

    own_rows = pl.ds(pl.multiple_of(pl.program_id(0) * rows, rows), rows)

    def second_stage(p, _):
        held = []

        def emit(j, center, near, far):
            total = diag[p + 2, :, piece(j)] * center + NEAR * near + FAR * far
            total = 2.0 * total - field[p + planes, :, piece(j)]
            if not last:
                out[p, :, piece(j)] = total
                return
            held.append(2.0 * total - first[p, :, piece(j)])
            if len(held) == GROUPS:
                done = split_groups(held, odd, upper)
                for a in range(GROUPS):
                    held_all[GROUPS * p + a, own_rows, piece(j // GROUPS)] = done[a]
                held.clear()

        stencil_row(inner, p, masks, emit)
        return 0

    lax.fori_loop(0, planes, second_stage, 0)
    if not last:
        pack_halo(out, place[2], to_mate, to_other)
        return

    @pl.when(pl.program_id(0) == pl.num_programs(0) - 1)
    def _():
        def one_part(i, _):
            both = [x[i].astype(jnp.float32) for x in done] + [held_all[i]]
            out[i] = jnp.concatenate(both, axis=0).astype(jnp.bfloat16)
            return 0

        lax.fori_loop(0, out.shape[0], one_part, 0)


def two_steps(place, halo, own, potential, partial, first=None, done=(), extra=False):
    planes, count, columns = own.shape
    last = first is not None
    spec = pl.BlockSpec((planes, ROWS, columns), lambda i: (0, i, 0))
    near = halo_shape(count, columns)
    out_shape = [jax.ShapeDtypeStruct(own.shape, own.dtype), near, near]
    out_spec = [spec, whole_spec(near.shape), whole_spec(near.shape)]
    ends = []
    if extra:
        diagonal = jax.ShapeDtypeStruct((planes + 4, columns), jnp.float32)
        out_shape.append(diagonal)
        out_spec.append(whole_spec(diagonal.shape))
        width = columns // GROUPS
        ends = [pl.BlockSpec((x.shape[0], width), lambda i, n=x.shape[1] // width: (0, n - 1)) for x in halo]
    scratch = [
        pltpu.VMEM((planes * 3, ROWS, columns), jnp.float32),
        pltpu.VMEM((planes + 4, ROWS, columns), jnp.float32),
        pltpu.VMEM((planes + 4, ROWS, columns), jnp.float32),
    ]
    if last:
        shape = (planes * GROUPS, count, columns // GROUPS)
        scratch.append(pltpu.VMEM(shape, jnp.float32))
        shape = (planes * GROUPS, count + sum(x.shape[1] for x in done), columns // GROUPS)
        out_shape = jax.ShapeDtypeStruct(shape, jnp.bfloat16)
        out_spec = pl.BlockSpec(shape, lambda i: (0, 0, 0))
    return pl.pallas_call(
        functools.partial(two_steps_kernel, last, extra, len(done)),
        grid=(count // ROWS,),
        in_specs=[whole_spec(x.shape) for x in done]
        + [pl.BlockSpec(memory_space=pltpu.SMEM)]
        + [whole_spec(halo[0].shape), spec, whole_spec(halo[1].shape), whole_spec(potential.shape), spec]
        + ends
        + [spec] * last,
        out_specs=out_spec,
        out_shape=out_shape,
        scratch_shapes=scratch,
        compiler_params=pltpu.CompilerParams(vmem_limit_bytes=VMEM_LIMIT),
        cost_estimate=pl.CostEstimate(flops=1, bytes_accessed=1, transcendentals=0),
    )(*done, place, halo[0], own, halo[1], potential, partial, *(halo if extra else ()), *([first] if last else []))


def z_order():
    one = np.zeros((NZ, NZ), np.float32)
    for z in range(NZ):
        one[z % ZI * ZB + z // ZI, z] = 1.0
    return jnp.asarray(np.kron(np.eye(GROUPS, dtype=np.float32), one), jnp.bfloat16)


def rotate_kernel(weights, cells, order, out):
    for k in range(cells.shape[1] // ROW_BLOCK):
        at = pl.ds(k * ROW_BLOCK, ROW_BLOCK)
        summed = jnp.dot(weights[...], cells[:, at], preferred_element_type=jnp.float32).astype(jnp.bfloat16)
        out[:, at] = jnp.dot(summed, order[...], preferred_element_type=jnp.float32).astype(jnp.bfloat16)


def rotate(weights, cells):
    return pl.pallas_call(
        rotate_kernel,
        out_shape=jax.ShapeDtypeStruct((weights.shape[0], cells.shape[1]), jnp.bfloat16),
        compiler_params=pltpu.CompilerParams(vmem_limit_bytes=VMEM_LIMIT),
        cost_estimate=pl.CostEstimate(flops=1, bytes_accessed=1, transcendentals=0),
    )(weights, cells, z_order())


def from_parts_kernel(parts, out, mixed):
    rows, planes, columns = out.shape
    width = parts.shape[2]
    groups = columns // width
    for p in range(planes):
        for a in range(groups):
            x = parts[p * groups + a].astype(jnp.float32)
            for j in range(width // LANE):
                for o in range(0, rows, ROWS):
                    at = pl.ds(o * planes + p, ROWS, stride=planes)
                    mixed[a * (width // LANE) + j, at, :] = x[o : o + ROWS, j * LANE : (j + 1) * LANE]
    for j in range(columns // LANE):
        out[:, :, piece(j)] = mixed[j].reshape(rows, planes, LANE)


def from_parts(parts, planes):
    n, count, width = parts.shape
    columns = n // planes * width
    return pl.pallas_call(
        from_parts_kernel,
        grid=(1,),
        in_specs=[pl.BlockSpec(parts.shape, lambda i: (0, 0, 0))],
        out_specs=pl.BlockSpec((count, planes, columns), lambda i: (0, 0, 0)),
        out_shape=jax.ShapeDtypeStruct((count, planes, columns), jnp.float32),
        scratch_shapes=[pltpu.VMEM((columns // LANE, count * planes, LANE), jnp.float32)],
        compiler_params=pltpu.CompilerParams(vmem_limit_bytes=VMEM_LIMIT),
        cost_estimate=pl.CostEstimate(flops=1, bytes_accessed=1, transcendentals=0),
    )(parts)


def body(orbitals, potential, rotation):
    count, planes, columns = orbitals.shape
    domains = lax.axis_size("space")
    members = lax.axis_size("band")
    mates = [(i, i ^ 1) for i in range(domains)]
    others = [(i, i + 1) for i in range(1, domains - 1, 2)]
    others = others + [(j, i) for i, j in others]

    def around(to_mate, to_other):
        other = lax.ppermute(to_other, "space", others)
        return lax.ppermute(to_mate, "space", mates), other

    at = lax.axis_index("space")
    place = jnp.stack([at > 0, at < domains - 1, at % 2]).astype(jnp.int32)

    orbitals = pltpu.with_memory_space_constraint(orbitals, pltpu.HBM)
    potential = pltpu.with_memory_space_constraint(potential, pltpu.HBM)
    starts = [sum(CHUNKS[:i]) for i in range(len(CHUNKS))]
    zeroth, halos = [], []
    for i, (start, chunk) in enumerate(zip(starts, CHUNKS)):
        fields, *halo = to_runs(place, orbitals, start, chunk, potential if i == 0 else None)
        if i == 0:
            field = halo.pop()
        zeroth.append(fields)
        halos.append(around(*halo))

    runs = field
    partials = [own_part(runs, x) for x in zeroth]
    fields_0, waited = lax.optimization_barrier((zeroth[0], halos[1][0]))
    halos[1] = (waited, halos[1][1])
    field = runs
    second, next_halos = [], []
    for i, (halo, fields, partial) in enumerate(zip(halos, (fields_0, zeroth[1]), partials)):
        fields, *halo = two_steps(place, halo, fields, field, partial, extra=i == 0)
        if i == 0:
            field = halo.pop()
        second.append(fields)
        next_halos.append(around(*halo))
    partials = [own_part(runs, x) for x in second]
    filtered = ()
    for fields, halo, partial, first in zip(second, next_halos, partials, zeroth):
        filtered = (two_steps(place, halo, fields, field, partial, first, filtered),)
    filtered, = filtered
    gathered = lax.all_to_all(filtered, "band", 0, 0)
    width = columns // GROUPS
    summed = rotate(rotation.T, gathered.reshape(members * count, width))
    back = lax.all_to_all(summed.reshape(members, count, width), "band", 0, 0)
    return from_parts(back, planes)


def solution(mesh):
    return jax.shard_map(
        body,
        mesh=mesh,
        in_specs=(P("band", "space", None), P("space", None), P()),
        out_specs=P("band", "space", None),
        check_vma=False,
    )
```

```python
import functools

import jax
import jax.numpy as jnp
import numpy as np
from jax import lax
from jax.experimental import pallas as pl
from jax.experimental.pallas import tpu as pltpu
from jax.sharding import PartitionSpec as P

NY = 48
NZ = 96
LANE = 128
ROWS = 8
GROUPS = 4
RUNS = NY // GROUPS
ZI = 3
ZB = NZ // ZI
PIECES = RUNS * ZI
TERMS = 5
ROW_BLOCK = GROUPS * NZ
VMEM_LIMIT = 14 * 1024 * 1024
CHUNKS = (16, 8)

CENTER = 4.75
HALF_WIDTH = 3.75
NEAR = -2.0 / 3.0 / HALF_WIDTH
FAR = 1.0 / 24.0 / HALF_WIDTH


def lanes_of(rows):
    return lax.broadcasted_iota(jnp.int32, (rows, LANE), 1)


def piece(j):
    return pl.ds(j * LANE, LANE)


def split_groups(four, odd, upper):
    half = {}
    for i in (0, 2):
        half[i] = jnp.where(odd, pltpu.roll(four[i + 1], ZB, 1), four[i])
        half[i + 1] = jnp.where(odd, four[i + 1], pltpu.roll(four[i], LANE - ZB, 1))
    done = {}
    for i in (0, 1):
        done[i] = jnp.where(upper, pltpu.roll(half[i + 2], 2 * ZB, 1), half[i])
        done[i + 2] = jnp.where(upper, half[i + 2], pltpu.roll(half[i], 2 * ZB, 1))
    return done


def rounded(x):
    return x.astype(jnp.bfloat16).astype(jnp.float32)


def pack_halo(planes, odd, to_mate, to_other):
    half = PIECES // 2
    base = pl.program_id(0) * (TERMS * half * LANE)

    def put(to, term, j, low, high):
        at = pl.ds(pl.multiple_of(base + (term * half + j) * LANE, LANE), LANE)
        to[:, at] = jnp.concatenate([low, high], axis=0).astype(jnp.bfloat16)

    for to, upward in ((to_mate, 1 - odd), (to_other, odd)):
        order = [jnp.where(upward == 1, 3 - k, k) for k in range(4)]
        for j in range(half):
            for k, p in enumerate(order):
                low, high = planes[p, :, piece(j)], planes[p, :, piece(j + half)]
                put(to, k + min(k, 1), j, low, high)
                if k == 0:
                    put(to, 1, j, low - rounded(low), high - rounded(high))


def unpack_halo(halo, below, field):
    half = PIECES // 2
    base = pl.program_id(0) * (TERMS * half * LANE)
    order = [jnp.where(below == 1, 3 - k, 8 + k) for k in range(4)]

    def get(term, j):
        at = pl.ds(pl.multiple_of(base + (term * half + j) * LANE, LANE), LANE)
        return halo[:, at].astype(jnp.float32)

    for j in range(half):
        for k, p in enumerate(order):
            both = get(0, j) + get(1, j) if k == 0 else get(k + 1, j)
            field[p, :, piece(j)] = both[:ROWS]
            field[p, :, piece(j + half)] = both[ROWS:]


def halo_shape(count, columns, extra=0):
    lanes = count // ROWS * TERMS * columns // 2 + extra * columns // GROUPS
    return jax.ShapeDtypeStruct((2 * ROWS, lanes), jnp.bfloat16)


def whole_spec(shape):
    return pl.BlockSpec(shape, lambda i: (0,) * len(shape))


def split_terms(x, terms, at):
    first = rounded(x)
    second = rounded(x - first)
    terms[0, at] = first.astype(jnp.bfloat16)
    terms[1, at] = second.astype(jnp.bfloat16)
    terms[2, at] = (x - first - second).astype(jnp.bfloat16)


def reordered(terms, order):
    _, count, width = terms.shape
    whole = jnp.dot(terms[...].reshape(3 * count, width), order[...], preferred_element_type=jnp.float32)
    return whole[:count] + (whole[count : 2 * count] + whole[2 * count :])


def potential_to_runs(cells, odd, order, out, to_mate, to_other, gathered, terms, quarters):
    planes, columns = cells.shape
    blocks = columns // ROW_BLOCK
    for k in range(blocks):
        x = cells[:, pl.ds(k * ROW_BLOCK, ROW_BLOCK)]
        gathered[pl.ds(k * ROWS, ROWS), :] = jnp.concatenate([x, jnp.zeros_like(x)], axis=0)
    split_terms(gathered[...], terms, pl.ds(0, blocks * ROWS))
    gathered[...] = reordered(terms, order)
    group = lanes_of(ROWS) // ZB
    per_group = blocks // GROUPS
    for m in range(PIECES // GROUPS):
        four = [gathered[pl.ds((a * per_group + m // ZI) * ROWS, ROWS), piece(m % ZI)] for a in range(GROUPS)]
        done = split_groups(four, group % 2 == 1, group >= 2)
        for i in range(GROUPS):
            x = done[i]
            j = GROUPS * m + i
            out[:, piece(j)] = x[:planes]
            quarter, lanes = j // (PIECES // GROUPS), piece(j % (PIECES // GROUPS))
            for to, upward in ((0, 1 - odd), (1, odd)):
                near = jnp.where(upward == 1, x[planes - 1 : planes], x[0:1])
                next_near = jnp.where(upward == 1, x[planes - 2 : planes - 1], x[1:2])
                rows = [near, near - rounded(near), next_near, next_near - rounded(next_near)]
                for r, row in enumerate(rows):
                    quarters[to, GROUPS * r + quarter : GROUPS * r + quarter + 1, lanes] = row
    width = columns // GROUPS
    for i, to in enumerate((to_mate, to_other)):
        to[:, to.shape[1] - width : to.shape[1]] = quarters[i].astype(jnp.bfloat16)


def to_runs_kernel(extra, place, cells, *rest):
    if extra:
        potential, out, to_mate, to_other, runs, order, terms, turned, gathered, few_terms, quarters = rest
    else:
        out, to_mate, to_other, order, terms, turned = rest
    planes, rows, columns = out.shape
    blocks = columns // ROW_BLOCK

    @pl.when(pl.program_id(0) == 0)
    def _():
        to = lax.broadcasted_iota(jnp.int32, order.shape, 1)
        source = to // NZ * NZ + to % ZB * ZI + to % NZ // ZB
        order[...] = jnp.where(lax.broadcasted_iota(jnp.int32, order.shape, 0) == source, 1.0, 0.0).astype(jnp.bfloat16)
        if extra:
            potential_to_runs(potential, place[2], order, runs, to_mate, to_other, gathered, few_terms, quarters)

    for k in range(blocks):
        x = cells[:, :, pl.ds(k * ROW_BLOCK, ROW_BLOCK)].reshape(rows * planes, ROW_BLOCK)
        split_terms(x, terms, pl.ds(k * rows * planes, rows * planes))
    whole = reordered(terms, order)
    for zi in range(ZI):
        turned[zi] = whole[:, zi * LANE : (zi + 1) * LANE]

    group = lanes_of(rows) // ZB
    odd = group % 2 == 1
    upper = group >= 2
    per_group = blocks // GROUPS
    for m in range(PIECES // GROUPS):
        for p in range(planes):
            four = []
            for a in range(GROUPS):
                k = a * per_group + m // ZI
                four.append(turned[m % ZI, pl.ds(k * rows * planes + p, rows, stride=planes), :])
            done = split_groups(four, odd, upper)
            for i in range(GROUPS):
                out[p, :, piece(GROUPS * m + i)] = done[i]
    pack_halo(out, place[2], to_mate, to_other)


def to_runs(place, cells, start, count, potential=None):
    _, planes, columns = cells.shape
    extra = potential is not None
    halo = halo_shape(count, columns, int(extra))
    blocks = columns // ROW_BLOCK
    total = planes * ROWS * blocks
    scratch = [
        pltpu.VMEM((ROW_BLOCK, ROW_BLOCK), jnp.bfloat16),
        pltpu.VMEM((3, total, ROW_BLOCK), jnp.bfloat16),
        pltpu.VMEM((ZI, total, LANE), jnp.float32),
    ]
    if extra:
        scratch.append(pltpu.VMEM((blocks * ROWS, ROW_BLOCK), jnp.float32))
        scratch.append(pltpu.VMEM((3, blocks * ROWS, ROW_BLOCK), jnp.bfloat16))
        scratch.append(pltpu.VMEM((2, 4 * GROUPS, columns // GROUPS), jnp.float32))
    return pl.pallas_call(
        functools.partial(to_runs_kernel, extra),
        grid=(count // ROWS,),
        in_specs=[
            pl.BlockSpec(memory_space=pltpu.SMEM),
            pl.BlockSpec((ROWS, planes, columns), lambda i: (start // ROWS + i, 0, 0)),
        ]
        + [whole_spec((planes, columns))] * extra,
        out_specs=[pl.BlockSpec((planes, ROWS, columns), lambda i: (0, i, 0))]
        + [whole_spec(halo.shape)] * 2
        + [whole_spec((planes, columns))] * extra,
        out_shape=[pltpu.HBM((planes, count, columns), cells.dtype), halo, halo]
        + [jax.ShapeDtypeStruct((planes, columns), jnp.float32)] * extra,
        scratch_shapes=scratch,
        compiler_params=pltpu.CompilerParams(vmem_limit_bytes=VMEM_LIMIT),
        cost_estimate=pl.CostEstimate(flops=1, bytes_accessed=1, transcendentals=0),
    )(place, cells, *([potential] if extra else []))


def stencil_row(src, plane, masks, emit):
    a_last, a_first, zb_last, zb_first = masks
    centers, turned = {}, {}

    def center(b, zi):
        if (b, zi) not in centers:
            centers[b, zi] = src[plane + 2, :, piece(ZI * b + zi)]
        return centers[b, zi]

    def turn(b, zi, by, mask):
        if (b, zi, by) not in turned:
            turned[b, zi, by] = jnp.where(mask, 0.0, pltpu.roll(center(b, zi), by, 1))
        return turned[b, zi, by]

    def at_y(b, zi):
        if b < 0:
            return turn(b + RUNS, zi, ZB, a_first)
        if b >= RUNS:
            return turn(b - RUNS, zi, LANE - ZB, a_last)
        return center(b, zi)

    def at_z(b, zi):
        if zi < 0:
            return turn(b, zi + ZI, 1, zb_first)
        if zi >= ZI:
            return turn(b, zi - ZI, LANE - 1, zb_last)
        return center(b, zi)

    def at_x(j, k):
        return src[plane + 2 + k, :, piece(j)]

    for b in range(RUNS):
        for zi in range(ZI):
            j = ZI * b + zi
            near, far = [
                (at_x(j, -k) + at_x(j, k)) + (at_y(b - k, zi) + at_y(b + k, zi)) + (at_z(b, zi - k) + at_z(b, zi + k))
                for k in (1, 2)
            ]
            emit(j, center(b, zi), near, far)


def potential_field_kernel(place, from_mate, own, from_other, out):
    planes = own.shape[0]
    scale = scaled_potential
    out[2 : planes + 2] = scale(own[...])
    mate, other = [halo[...].astype(jnp.float32) for halo in (from_mate, from_other)]
    mate_below = place[2] == 1
    below = jnp.where(mate_below, mate, other)
    above = jnp.where(mate_below, other, mate)
    width = below.shape[1]
    rows = ((1, below, 0), (0, below, 2), (planes + 2, above, 0), (planes + 3, above, 2))
    for p, terms, first in rows:
        whole = terms[first * GROUPS : (first + 1) * GROUPS] + terms[(first + 1) * GROUPS : (first + 2) * GROUPS]
        for q in range(GROUPS):
            out[p : p + 1, q * width : (q + 1) * width] = scale(whole[q : q + 1])


def scaled_potential(x):
    return (x + (HALF_WIDTH - CENTER)) / HALF_WIDTH


def shift_masks(rows):
    lane = lanes_of(rows)
    return lane >= LANE - ZB, lane < ZB, lane % ZB == ZB - 1, lane % ZB == 0


def own_part_kernel(potential, own, out, field, diag):
    planes, rows, columns = own.shape

    @pl.when(pl.program_id(0) == 0)
    def _():
        for p in (0, 1, planes + 2, planes + 3):
            field[p] = jnp.zeros((rows, columns), jnp.float32)
        for p in range(planes):
            diag[p] = jnp.broadcast_to(scaled_potential(potential[p : p + 1, :]), (rows, columns))

    field[2 : planes + 2] = own[...]
    masks = shift_masks(rows)

    def one_plane(p, _):
        def emit(j, center, near, far):
            out[p, :, piece(j)] = diag[p, :, piece(j)] * center + NEAR * near + FAR * far

        stencil_row(field, p, masks, emit)
        return 0

    lax.fori_loop(0, planes, one_plane, 0)


def own_part(potential, own):
    planes, count, columns = own.shape
    spec = pl.BlockSpec((planes, ROWS, columns), lambda i: (0, i, 0))
    return pl.pallas_call(
        own_part_kernel,
        grid=(count // ROWS,),
        in_specs=[whole_spec(potential.shape), spec],
        out_specs=spec,
        out_shape=jax.ShapeDtypeStruct(own.shape, own.dtype),
        scratch_shapes=[
            pltpu.VMEM((planes + 4, ROWS, columns), jnp.float32),
            pltpu.VMEM((planes, ROWS, columns), jnp.float32),
        ],
        compiler_params=pltpu.CompilerParams(vmem_limit_bytes=VMEM_LIMIT),
        cost_estimate=pl.CostEstimate(flops=1, bytes_accessed=1, transcendentals=0),
    )(potential, own)


def two_steps_kernel(last, extra, count_done, *refs):
    done = refs[:count_done]
    place, from_mate, own, from_other, potential, partial, *rest = refs[count_done:]
    if extra:
        runs, (mate_end, other_end, out, to_mate, to_other, potential, *rest) = potential, rest
        rest = (out, to_mate, to_other, *rest)
    if last:
        first, out, field, inner, diag, held_all = rest
    else:
        out, to_mate, to_other, field, inner, diag = rest
    planes, rows, columns = own.shape

    @pl.when(pl.program_id(0) == 0)
    def _():
        if extra:
            potential_field_kernel(place, mate_end, runs, other_end, potential)
        for p in range(planes + 4):
            diag[p] = jnp.broadcast_to(potential[p : p + 1, :], (rows, columns))

    unpack_halo(from_mate, place[2], field)
    field[planes : 2 * planes] = own[...]
    unpack_halo(from_other, 1 - place[2], field)

    masks = shift_masks(rows)
    group = lanes_of(rows) // ZB
    odd = group % 2 == 1
    upper = group >= 2

    def first_stage(q, _):
        p = q + jnp.where(q >= 2, planes, 0)
        here = jnp.where(q < 2, place[0], place[1]).astype(jnp.float32)
        near_by = here * NEAR
        far_by = here * FAR

        def emit(j, center, near, far):
            inner[p, :, piece(j)] = diag[p, :, piece(j)] * center + near_by * near + far_by * far

        stencil_row(field, p + planes - 4, masks, emit)
        return 0

    lax.fori_loop(0, 4, first_stage, 0)
    top = 2 * planes
    for at in range(0, columns, ROW_BLOCK):
        lanes = pl.ds(at, ROW_BLOCK)
        below = field[planes - 1, :, lanes]
        above = field[top, :, lanes]
        inner[2, :, lanes] = partial[0, :, lanes] + (NEAR * below + FAR * field[planes - 2, :, lanes])
        inner[3, :, lanes] = partial[1, :, lanes] + FAR * below
        inner[planes, :, lanes] = partial[planes - 2, :, lanes] + FAR * above
        inner[planes + 1, :, lanes] = partial[planes - 1, :, lanes] + (NEAR * above + FAR * field[top + 1, :, lanes])

    own_rows = pl.ds(pl.multiple_of(pl.program_id(0) * rows, rows), rows)

    def second_stage(p, _):
        held = []

        def emit(j, center, near, far):
            total = diag[p + 2, :, piece(j)] * center + NEAR * near + FAR * far
            total = 2.0 * total - field[p + planes, :, piece(j)]
            if not last:
                out[p, :, piece(j)] = total
                return
            held.append(2.0 * total - first[p, :, piece(j)])
            if len(held) == GROUPS:
                done = split_groups(held, odd, upper)
                for a in range(GROUPS):
                    held_all[GROUPS * p + a, own_rows, piece(j // GROUPS)] = done[a]
                held.clear()

        stencil_row(inner, p, masks, emit)
        return 0

    lax.fori_loop(0, planes, second_stage, 0)
    if not last:
        pack_halo(out, place[2], to_mate, to_other)
        return

    @pl.when(pl.program_id(0) == pl.num_programs(0) - 1)
    def _():
        def one_part(i, _):
            both = [x[i].astype(jnp.float32) for x in done] + [held_all[i]]
            out[i] = jnp.concatenate(both, axis=0).astype(jnp.bfloat16)
            return 0

        lax.fori_loop(0, out.shape[0], one_part, 0)


def two_steps(place, halo, own, potential, partial, first=None, done=(), extra=False):
    planes, count, columns = own.shape
    last = first is not None
    spec = pl.BlockSpec((planes, ROWS, columns), lambda i: (0, i, 0))
    near = halo_shape(count, columns)
    out_shape = [jax.ShapeDtypeStruct(own.shape, own.dtype), near, near]
    out_spec = [spec, whole_spec(near.shape), whole_spec(near.shape)]
    ends = []
    if extra:
        diagonal = jax.ShapeDtypeStruct((planes + 4, columns), jnp.float32)
        out_shape.append(diagonal)
        out_spec.append(whole_spec(diagonal.shape))
        width = columns // GROUPS
        ends = [pl.BlockSpec((x.shape[0], width), lambda i, n=x.shape[1] // width: (0, n - 1)) for x in halo]
    scratch = [
        pltpu.VMEM((planes * 3, ROWS, columns), jnp.float32),
        pltpu.VMEM((planes + 4, ROWS, columns), jnp.float32),
        pltpu.VMEM((planes + 4, ROWS, columns), jnp.float32),
    ]
    if last:
        shape = (planes * GROUPS, count, columns // GROUPS)
        scratch.append(pltpu.VMEM(shape, jnp.float32))
        shape = (planes * GROUPS, count + sum(x.shape[1] for x in done), columns // GROUPS)
        out_shape = jax.ShapeDtypeStruct(shape, jnp.bfloat16)
        out_spec = pl.BlockSpec(shape, lambda i: (0, 0, 0))
    return pl.pallas_call(
        functools.partial(two_steps_kernel, last, extra, len(done)),
        grid=(count // ROWS,),
        in_specs=[whole_spec(x.shape) for x in done]
        + [pl.BlockSpec(memory_space=pltpu.SMEM)]
        + [whole_spec(halo[0].shape), spec, whole_spec(halo[1].shape), whole_spec(potential.shape), spec]
        + ends
        + [spec] * last,
        out_specs=out_spec,
        out_shape=out_shape,
        scratch_shapes=scratch,
        compiler_params=pltpu.CompilerParams(vmem_limit_bytes=VMEM_LIMIT),
        cost_estimate=pl.CostEstimate(flops=1, bytes_accessed=1, transcendentals=0),
    )(*done, place, halo[0], own, halo[1], potential, partial, *(halo if extra else ()), *([first] if last else []))


def z_order():
    one = np.zeros((NZ, NZ), np.float32)
    for z in range(NZ):
        one[z % ZI * ZB + z // ZI, z] = 1.0
    return jnp.asarray(np.kron(np.eye(GROUPS, dtype=np.float32), one), jnp.bfloat16)


def rotate_kernel(weights, cells, order, out):
    for k in range(cells.shape[1] // ROW_BLOCK):
        at = pl.ds(k * ROW_BLOCK, ROW_BLOCK)
        summed = jnp.dot(weights[...], cells[:, at], preferred_element_type=jnp.float32).astype(jnp.bfloat16)
        out[:, at] = jnp.dot(summed, order[...], preferred_element_type=jnp.float32).astype(jnp.bfloat16)


def rotate(weights, cells):
    return pl.pallas_call(
        rotate_kernel,
        out_shape=jax.ShapeDtypeStruct((weights.shape[0], cells.shape[1]), jnp.bfloat16),
        compiler_params=pltpu.CompilerParams(vmem_limit_bytes=VMEM_LIMIT),
        cost_estimate=pl.CostEstimate(flops=1, bytes_accessed=1, transcendentals=0),
    )(weights, cells, z_order())


def from_parts_kernel(parts, out, mixed):
    rows, planes, columns = out.shape
    width = parts.shape[2]
    groups = columns // width
    for p in range(planes):
        for a in range(groups):
            x = parts[p * groups + a].astype(jnp.float32)
            for j in range(width // LANE):
                for o in range(0, rows, ROWS):
                    at = pl.ds(o * planes + p, ROWS, stride=planes)
                    mixed[a * (width // LANE) + j, at, :] = x[o : o + ROWS, j * LANE : (j + 1) * LANE]
    for j in range(columns // LANE):
        out[:, :, piece(j)] = mixed[j].reshape(rows, planes, LANE)


def from_parts(parts, planes):
    n, count, width = parts.shape
    columns = n // planes * width
    return pl.pallas_call(
        from_parts_kernel,
        grid=(1,),
        in_specs=[pl.BlockSpec(parts.shape, lambda i: (0, 0, 0))],
        out_specs=pl.BlockSpec((count, planes, columns), lambda i: (0, 0, 0)),
        out_shape=jax.ShapeDtypeStruct((count, planes, columns), jnp.float32),
        scratch_shapes=[pltpu.VMEM((columns // LANE, count * planes, LANE), jnp.float32)],
        compiler_params=pltpu.CompilerParams(vmem_limit_bytes=VMEM_LIMIT),
        cost_estimate=pl.CostEstimate(flops=1, bytes_accessed=1, transcendentals=0),
    )(parts)


def body(orbitals, potential, rotation):
    count, planes, columns = orbitals.shape
    domains = lax.axis_size("space")
    members = lax.axis_size("band")
    mates = [(i, i ^ 1) for i in range(domains)]
    others = [(i, i + 1) for i in range(1, domains - 1, 2)]
    others = others + [(j, i) for i, j in others]

    def around(to_mate, to_other):
        other = lax.ppermute(to_other, "space", others)
        return lax.ppermute(to_mate, "space", mates), other

    at = lax.axis_index("space")
    place = jnp.stack([at > 0, at < domains - 1, at % 2]).astype(jnp.int32)

    orbitals = pltpu.with_memory_space_constraint(orbitals, pltpu.HBM)
    potential = pltpu.with_memory_space_constraint(potential, pltpu.HBM)
    starts = [sum(CHUNKS[:i]) for i in range(len(CHUNKS))]
    zeroth, halos = [], []
    for i, (start, chunk) in enumerate(zip(starts, CHUNKS)):
        fields, *halo = to_runs(place, orbitals, start, chunk, potential if i == 0 else None)
        if i == 0:
            field = halo.pop()
        zeroth.append(fields)
        halos.append(around(*halo))

    runs = field
    partials = [own_part(runs, x) for x in zeroth]
    fields_0, waited = lax.optimization_barrier((zeroth[0], halos[1][0]))
    halos[1] = (waited, halos[1][1])
    field = runs
    second, next_halos = [], []
    for i, (halo, fields, partial) in enumerate(zip(halos, (fields_0, zeroth[1]), partials)):
        fields, *halo = two_steps(place, halo, fields, field, partial, extra=i == 0)
        if i == 0:
            field = halo.pop()
        second.append(fields)
        next_halos.append(around(*halo))
    partials = [own_part(runs, x) for x in second]
    filtered = ()
    for fields, halo, partial, first in zip(second, next_halos, partials, zeroth):
        filtered = (two_steps(place, halo, fields, field, partial, first, filtered),)
    filtered, = filtered
    gathered = lax.all_to_all(filtered, "band", 0, 0)
    width = columns // GROUPS
    summed = rotate(rotation.T, gathered.reshape(members * count, width))
    back = lax.all_to_all(summed.reshape(members, count, width), "band", 0, 0)
    return from_parts(back, planes)


def solution(mesh):
    return jax.shard_map(
        body,
        mesh=mesh,
        in_specs=(P("band", "space", None), P("space", None), P()),
        out_specs=P("band", "space", None),
        check_vma=False,
    )
```
